256 devices in a mesh: patch: 64 (over z, y, core), band: 4 (over x).
Axes of the slice: x: 4, y: 4, z: 8, core: 2. Of those that a mesh axis runs over, the one named last changes fastest.
Arguments:
- exposures: float32 [512, 256, 128], P(('band', 'patch')), parts along dimension 0, may hold values from -6 to 6
- variance: float32 [512, 256, 128], P(('band', 'patch')), parts along dimension 0, may hold values from 0.01 to 60, as said below
- mask_bits: int32 [512, 256, 128], P(('band', 'patch')), parts along dimension 0, may hold values from 0 to 4095
- kernel_coeffs: float32 [512, 27, 6], P(('band', 'patch')), parts along dimension 0, may hold values from -3 to 3
- ccd_visit: int32 [512, 1], P(('band', 'patch')), parts along dimension 0, may hold values from 0 to 7
- strip_patch: int32 [16384, 1], P(('band', 'patch')), parts along dimension 0, may hold values from 0 to 63, as said below
- strip_row: int32 [16384], P(('band', 'patch')), parts along dimension 0, may hold values from 0 to 120
- strip_col: int32 [16384], P(('band', 'patch')), parts along dimension 0, may hold values from 0 to 384
Outputs:
- coadd_image: float32 [256, 128, 512], P(('band', 'patch')), parts along dimension 0
- weight_map: float32 [256, 128, 512], P(('band', 'patch')), parts along dimension 0
The draws below stay inside these ranges and needn't reach their ends.
There are 4 independent parts, one for each index of `band`. The reference program is written for one: setup_inputs(seed, part) draws one part's arguments, and reference() takes and returns one part's arrays. A program takes and returns all parts, laid end to end along the dimension named above; each array names one. Nothing has to cross between parts.
Inputs may be any that keep to these rules, and one draw needn't show every extreme that they name: `variance`: Positive. `ccd_visit`: every visit has at least one CCD. `strip_patch`: among the strips of one device (aligned blocks of 64 rows) no patch is named more than 2 times; one patch is named exactly 2 times in every block.
All inputs are finite; a program needn't handle non-finite values.
Results may differ from the reference program's by a relative error of at most 0.00011.
Values sent between devices are 32-bit elements; how exact they have to be, the bound alone decides.
A program may use at most 64 MiB of HBM per device.

```python
import jax
import jax.numpy as jnp
from jax import lax

CH = 256
CW = 128
SR = 8
PH = 128
PW = 512
KS = 21
NB = 27
NSP = 6
VISITS = 8
CCDS = 128
STRIPS_DEV = 64
STRIPS = 4096
PATCHES = 64
CAP = 2


def draw_variance(key, part):
    row_key, column_key, pixel_key = jax.random.split(jax.random.fold_in(key, 7), 3)
    ten_log = jnp.log(10.0)
    row_scale = jnp.exp(jax.random.uniform(row_key, (CCDS, CH, 1), jnp.float32) * ten_log)
    column_scale = jnp.exp(jax.random.uniform(column_key, (CCDS, 1, CW), jnp.float32) * ten_log)
    position = jnp.arange(CCDS).astype(jnp.float32) / max(CCDS - 1, 1)
    increasing_order = 1.0 + 2.0 * position
    pixel_scale = jnp.exp(jax.random.uniform(pixel_key, (CCDS, CH, CW), jnp.float32, -0.7, 0.7))
    return 0.03 * increasing_order[:, None, None] * row_scale * column_scale * pixel_scale


def draw_strip_patch(key, part):
    hot_key, bias_key, block_key = jax.random.split(jax.random.fold_in(key, 13), 3)
    hot_patch = jax.random.randint(hot_key, (), 0, PATCHES)
    patch_bias = jax.random.randint(bias_key, (PATCHES,), 0, 4) * 1024
    copies = jnp.repeat(jnp.arange(PATCHES, dtype=jnp.int32), CAP)
    tie_break = jnp.arange(PATCHES * CAP, dtype=jnp.int32)

    def one_block(sub_key):
        noise_key, shuffle_key = jax.random.split(sub_key)
        noise = jax.random.randint(noise_key, (PATCHES * CAP,), 0, 4096)
        score = noise + patch_bias[copies] + (copies == hot_patch).astype(jnp.int32) * 65536
        score = score * (PATCHES * CAP) + tie_break
        chosen = copies[lax.top_k(score, STRIPS_DEV)[1]]
        return chosen[jax.random.permutation(shuffle_key, STRIPS_DEV)]
    blocks = jax.vmap(one_block)(jax.random.split(block_key, PATCHES))
    return blocks.reshape(STRIPS, 1).astype(jnp.int32)


def touch_ends(values, stream_key, smallest, high):
    dims = values.shape
    place = [jax.random.randint(jax.random.fold_in(stream_key, axis), (), 0, dims[axis]) for axis in range(len(dims))]
    values = values.at[tuple(place)].set(smallest)
    longest = dims.index(max(dims))
    place[longest] = (place[longest] + 1) % dims[longest]
    return values.at[tuple(place)].set(high)


def shard_levels(stream_key, shape, shards, smallest, top_value):
    def one(axis_at, parts):
        heights = jax.random.uniform(jax.random.fold_in(jax.random.fold_in(stream_key, 6), axis_at), (parts,), jnp.float32, smallest / len(shards), top_value / len(shards))
        return jnp.repeat(jnp.exp(heights), shape[axis_at] // parts).reshape((-1,) + (1,) * (len(shape) - axis_at - 1))

    level = one(*shards[0])
    for cut in shards[1:]:
        level = level * one(*cut)
    return level


def different_ones(stream_key, rows, amount, top, lift):
    sequence = jax.random.permutation(jax.random.fold_in(stream_key, 1), amount)
    favour = sequence
    for power in range(3):
        favour = favour * favour // amount
    favour = favour * lift // amount
    tickets = jax.random.randint(jax.random.fold_in(stream_key, 2), (rows, amount), 0, 4096) + favour
    fixed_rows = jax.random.permutation(jax.random.fold_in(stream_key, 3), rows)[jnp.arange(amount) % rows]
    tickets = jnp.where(jnp.arange(rows)[:, None] == fixed_rows[None, :], 1 << 14, tickets)
    score = tickets * amount + jnp.arange(amount)
    return lax.top_k(score.astype(jnp.int32), top)[1].astype(jnp.int32)


def scatter_about(rng, dims, width, most, cuts=(), held_as=jnp.bfloat16):
    values = jax.random.normal(rng, dims, jnp.float32) * width
    if len(cuts) > 0:
        values = shard_levels(rng, dims, cuts, -0.22, 0.18) * values
    return jnp.clip(values, min=-most, max=most).astype(held_as)


def setup_inputs(seed: int = 0, part: int = 0) -> dict:
    key_list = jax.random.split(jax.random.key(seed), 9)
    part_splits = jax.random.split(jax.random.fold_in(key_list[8], part), 9)
    return {
        "exposures": scatter_about(part_splits[0], (CCDS, CH, CW), 1.0, 6.0, ((0, 64),), jnp.float32),
        "variance": draw_variance(jax.random.fold_in(jax.random.fold_in(key_list[8], part), 71), part),
        "mask_bits": touch_ends(jax.random.randint(part_splits[2], (CCDS, CH, CW), 0, 4096), jax.random.fold_in(part_splits[2], 1), 0, 4095).astype(jnp.int32),
        "kernel_coeffs": scatter_about(part_splits[3], (CCDS, NB, NSP), 0.4, 3.0, ((0, 64),), jnp.float32),
        "ccd_visit": different_ones(part_splits[4], CCDS, VISITS, 1, 0),
        "strip_patch": draw_strip_patch(jax.random.fold_in(jax.random.fold_in(key_list[8], part), 71), part),
        "strip_row": touch_ends(jax.random.randint(part_splits[6], (STRIPS,), 0, PH - SR + 1), jax.random.fold_in(part_splits[6], 1), 0, PH - SR).astype(jnp.int32),
        "strip_col": touch_ends(jax.random.randint(part_splits[7], (STRIPS,), 0, PW - CW + 1), jax.random.fold_in(part_splits[7], 1), 0, PW - CW).astype(jnp.int32),
    }


gauss_widths = (0.75, 1.5, 3.0)
largest_value = lax.Precision.HIGHEST


def tap_values(offsets, kernel_half_width):
    support = jnp.arange(-kernel_half_width, kernel_half_width + 1).astype(jnp.float32)
    inside = (jnp.abs(offsets) <= kernel_half_width).astype(jnp.float32)
    tables = []
    for spread in gauss_widths:
        gauss_total = jnp.sum(jnp.exp(-support * support / (2.0 * spread * spread)))
        profile = jnp.exp(-offsets * offsets / (2.0 * spread * spread)) / gauss_total * inside
        scaled = offsets / spread
        tables.append(jnp.stack([profile, profile * scaled, profile * scaled * scaled]))
    return jnp.stack(tables)


def row_filters(row_count, kernel_half_width):
    row_ids = jnp.arange(row_count)[:, None]
    window_ids = jnp.arange(row_count + 2 * kernel_half_width)[None, :]
    return tap_values((window_ids - row_ids - kernel_half_width).astype(jnp.float32), kernel_half_width)


def column_filters(column_count, kernel_half_width):
    source = jnp.arange(column_count)[:, None]
    target_patch = jnp.arange(column_count)[None, :]
    return tap_values((source - target_patch).astype(jnp.float32), kernel_half_width)


def convolve(windows, kernel_terms, row_starts, height):
    kernel_half_width = KS // 2
    batch_size = windows.shape[0]
    row_count = windows.shape[1] - 2 * kernel_half_width
    columns = windows.shape[2]
    smooth = jnp.einsum('gaij,njc->ngaic', row_filters(row_count, kernel_half_width), windows, precision=largest_value)
    column_ops = column_filters(columns, kernel_half_width)
    row_coords = row_starts[:, None] + jnp.arange(row_count).astype(jnp.float32)[None, :]
    y_plane = jnp.broadcast_to((2.0 * row_coords / (height - 1) - 1.0)[:, :, None], (batch_size, row_count, columns))
    x_line = 2.0 * jnp.arange(columns).astype(jnp.float32) / (columns - 1) - 1.0
    x_plane = jnp.broadcast_to(x_line[None, None, :], (batch_size, row_count, columns))
    ones_plane = jnp.ones((batch_size, row_count, columns), jnp.float32)
    poly_planes = jnp.stack([ones_plane, x_plane, y_plane, x_plane * x_plane, x_plane * y_plane, y_plane * y_plane], axis=1)
    kernel_split = kernel_terms.reshape(batch_size, 3, 9, kernel_terms.shape[2])
    result = jnp.zeros((batch_size, row_count, columns), jnp.float32)
    for gauss_index in range(3):
        basis_images = jnp.einsum('naic,bcd->nabid', smooth[:, gauss_index], column_ops[gauss_index], precision=largest_value)
        fields = jnp.einsum('nkp,npid->nkid', kernel_split[:, gauss_index], poly_planes, precision=largest_value)
        fields = fields.reshape(batch_size, 3, 3, row_count, columns)
        result = result + jnp.sum(basis_images * fields, axis=(1, 2))
    return result


def reference(exposures, variance, mask_bits, kernel_coeffs, ccd_visit, strip_patch, strip_row, strip_col):
    kernel_half_width = KS // 2
    usable = (jnp.bitwise_and(mask_bits, 3) != 3).astype(jnp.float32)
    visit_hot = (ccd_visit == jnp.arange(VISITS).astype(jnp.int32)[None, :]).astype(jnp.float32)
    visit_count = jnp.sum(jnp.sum(usable, axis=(1, 2))[:, None] * visit_hot, axis=0)
    visit_load = jnp.sum(jnp.sum(usable * variance, axis=(1, 2))[:, None] * visit_hot, axis=0)
    visit_weight = (visit_count + 1.0) / (visit_load + 1.0)
    detector_weight = jnp.sum(visit_hot * visit_weight[None, :], axis=1)
    padded = jnp.pad(exposures, ((0, 0), (kernel_half_width, kernel_half_width), (0, 0)))

    def match_one(ccd_pair):
        return convolve(ccd_pair[0][None], ccd_pair[1][None], jnp.zeros((1,), jnp.float32), CH)[0]

    convolved = lax.map(match_one, (padded, kernel_coeffs))
    plane_weight = detector_weight[:, None, None] * usable
    flux_strips = (plane_weight * convolved).reshape(STRIPS, SR, CW)
    weight_strips = plane_weight.reshape(STRIPS, SR, CW)
    target_patch = jnp.broadcast_to(strip_patch[:, 0][:, None, None], (STRIPS, SR, CW))
    row_index = jnp.broadcast_to(strip_row[:, None, None] + jnp.arange(SR).astype(jnp.int32)[None, :, None], (STRIPS, SR, CW))
    col_index = jnp.broadcast_to(strip_col[:, None, None] + jnp.arange(CW).astype(jnp.int32)[None, None, :], (STRIPS, SR, CW))
    numerator = jnp.zeros((PATCHES, PH, PW), jnp.float32).at[target_patch, row_index, col_index].add(flux_strips)
    weight_map = jnp.zeros((PATCHES, PH, PW), jnp.float32).at[target_patch, row_index, col_index].add(weight_strips)
    coadd_image = numerator / jnp.maximum(weight_map, 1.0)
    return (coadd_image, weight_map)
```

```python
import functools

import jax
import jax.numpy as jnp
import numpy as np
from jax import lax
from jax.experimental import pallas as pl
from jax.experimental.pallas import tpu as pltpu
from jax.sharding import PartitionSpec as P

PH = 128
PW = 512
KS = 21
VISITS = 8
GAUSS_WIDTHS = (0.75, 1.5, 3.0)
MESH = pl.DeviceIdType.MESH
F32 = jnp.float32
BF16 = jnp.bfloat16

CCDS = 2
CH = 256
CW = 128
SR = 8
STRIPS = 64
DEVS = 64
SLOTS = 2
BLOCK = SLOTS * SR
PLANES = 8
GROUP = DEVS // PLANES
CHUNK = GROUP * BLOCK
COL_SHIFT = 192


def taps(offsets):
    half = KS // 2
    support = np.arange(-half, half + 1, dtype=np.float64)
    inside = np.abs(offsets) <= half
    tables = []
    for spread in GAUSS_WIDTHS:
        total = np.sum(np.exp(-support * support / (2.0 * spread * spread)))
        profile = np.where(inside, np.exp(-offsets * offsets / (2.0 * spread * spread)) / total, 0.0)
        scaled = offsets / spread
        tables += [profile, profile * scaled, profile * scaled * scaled]
    return np.stack(tables)


def tap_matrices():
    rows = np.arange(CH, dtype=np.float64)
    row_ops = taps(rows[None, :] - rows[:, None]).astype(np.float32).reshape(9 * CH, CH)
    cols = np.arange(CW, dtype=np.float64)
    col_ops = taps(cols[:, None] - cols[None, :]).astype(np.float32).reshape(9 * CW, CW)
    high = row_ops.astype(BF16)
    low = (row_ops - high.astype(np.float32)).astype(BF16)
    return high, low, col_ops


def split(x):
    high = x.astype(BF16)
    return high, (x - high.astype(F32)).astype(BF16)


def dot(a, b):
    return jnp.dot(a, b, preferred_element_type=F32)


def kernel(
    mask_h, var_h, exp_h, coef, visit_s, patch, row, col, col_s, rhi_h, rlo_h, cop_h,
    num_o, wgt_o,
    mask, var, expo, rhi, rlo, cop, use, tmp, e_hi, e_lo, s_hi, s_lo, m_hi, m_lo, wk,
    hot, wsend, fsend, msend, wrecv, frecv, mrecv, crep, vrep, rt, rhs, num, wgt,
    load_sem, send_sem, wsem, fsem, msem,
):
    me = lax.axis_index("patch")
    band = lax.axis_index("band")
    my_plane = me // GROUP

    loads = [
        pltpu.make_async_copy(src, dst, load_sem.at[k])
        for k, (src, dst) in enumerate(
            [(mask_h, mask), (var_h, var), (exp_h, expo), (rhi_h, rhi), (rlo_h, rlo), (cop_h, cop)]
        )
    ]
    for load in loads:
        load.start()

    barrier = pltpu.get_barrier_semaphore()

    def greet(k, c):
        pl.semaphore_signal(
            barrier, inc=1, device_id=(lax.rem(me + k, DEVS), band), device_id_type=MESH
        )
        return c

    lax.fori_loop(1, DEVS, greet, 0)

    lane = lax.broadcasted_iota(jnp.int32, (STRIPS, STRIPS), 1)
    sub = lax.broadcasted_iota(jnp.int32, (STRIPS, STRIPS), 0)
    prow = patch[...]
    pfull = jnp.broadcast_to(prow, (STRIPS, STRIPS))
    pcol = jnp.sum(jnp.where(lane == sub, pfull, 0), axis=1, keepdims=True)
    rank = jnp.sum(
        jnp.where((pcol == pfull) & (sub < lane), 1, 0), axis=0, keepdims=True
    )
    slot = prow * SLOTS + rank
    slot_id = lax.broadcasted_iota(jnp.int32, (DEVS * SLOTS, STRIPS), 0)
    hot[...] = (slot_id == slot).astype(F32).astype(BF16)

    def roll_strips(values):
        def one(s, c):
            at = pl.ds(pl.multiple_of(s * SR, SR), SR)
            tmp[at, :] = pltpu.roll(values[at, :], lax.bitwise_and(col_s[s], CW - 1), 1)
            return c

        lax.fori_loop(0, STRIPS, one, 0, unroll=8)

    loads[0].wait()
    use[...] = jnp.where(jnp.bitwise_and(mask[...], 3) != 3, 1.0, 0.0)
    roll_strips(use)
    for i in range(SR):
        wsend[pl.ds(i, DEVS * SLOTS, stride=SR), :] = dot(
            hot[...], tmp[pl.ds(i, STRIPS, stride=SR), :].astype(BF16)
        )

    pl.semaphore_wait(barrier, DEVS - 1)

    def block(d):
        return pl.ds(pl.multiple_of(d * BLOCK, BLOCK), BLOCK)

    def send_all(src, dst, ssem, rsem):
        def one(k, c):
            d = lax.rem(me + k, DEVS)
            pltpu.make_async_remote_copy(
                src_ref=src.at[block(d)],
                dst_ref=dst.at[block(me)],
                send_sem=ssem,
                recv_sem=rsem.at[my_plane],
                device_id=(d, band),
                device_id_type=MESH,
            ).start()
            return c

        lax.fori_loop(1, DEVS, one, 0)
        pltpu.make_async_copy(src.at[block(me)], dst.at[block(me)], rsem.at[my_plane]).start()

    send_all(wsend, wrecv, send_sem.at[0], wsem)

    loads[1].wait()
    lane1 = lax.broadcasted_iota(jnp.int32, (1, CW), 1)
    sums = jnp.zeros((1, CW), F32)
    for c in range(CCDS):
        u = use[c * CH : (c + 1) * CH, :]
        count = jnp.sum(u)
        amount = jnp.sum(u * var[c * CH : (c + 1) * CH, :])
        v = visit_s[c, 0]
        sums = sums + jnp.where(lane1 == v + 16, count, 0.0) + jnp.where(lane1 == v + 24, amount, 0.0)
    strip_lane = lax.broadcasted_iota(jnp.int32, (1, STRIPS), 1)
    vrow = jnp.where(strip_lane < STRIPS // CCDS, visit_s[0, 0], visit_s[1, 0])
    q_sub = lax.broadcasted_iota(jnp.int32, (CW, STRIPS), 0)
    hot_id = lax.broadcasted_iota(jnp.int32, (DEVS, STRIPS), 0)
    meta = jnp.broadcast_to(sums, (DEVS, CW))
    for j in range(SLOTS):
        q = jnp.where(q_sub == 8 * j, row[...], 0)
        q = jnp.where(q_sub == 8 * j + 1, col[...] - COL_SHIFT, q)
        q = jnp.where(q_sub == 8 * j + 2, vrow, q)
        hot_j = (hot_id * SLOTS + j == slot).astype(F32).astype(BF16)
        meta = meta + lax.dot_general(
            hot_j, q.astype(F32).astype(BF16), (((1,), (1,)), ((), ())), preferred_element_type=F32
        )
    msend[...] = meta.reshape(DEVS, 1, CW)

    def send_meta(k, c):
        d = lax.rem(me + k, DEVS)
        pltpu.make_async_remote_copy(
            src_ref=msend.at[d],
            dst_ref=mrecv.at[me],
            send_sem=send_sem.at[1],
            recv_sem=msem,
            device_id=(d, band),
            device_id_type=MESH,
        ).start()
        return c

    lax.fori_loop(1, DEVS, send_meta, 0)
    own_meta = pltpu.make_async_copy(msend.at[me], mrecv.at[me], load_sem.at[6])
    own_meta.start()

    loads[2].wait()
    for c in range(CCDS):
        high, low = split(expo[c * CH : (c + 1) * CH, :])
        e_hi[:, c * CW : (c + 1) * CW] = high
        e_lo[:, c * CW : (c + 1) * CW] = low
    loads[3].wait()
    loads[4].wait()

    def row_pass(k, c):
        at = pl.ds(pl.multiple_of(k * CH, CH), CH)
        to = pl.ds(pl.multiple_of(k * CW, CW), CW)
        s = dot(rhi[at, :], e_hi[...]) + dot(rhi[at, :], e_lo[...]) + dot(rlo[at, :], e_hi[...])
        high, low = split(s)
        for n in range(CCDS):
            s_hi[n, :, to] = high[:, n * CW : (n + 1) * CW]
            s_lo[n, :, to] = low[:, n * CW : (n + 1) * CW]
        return c

    lax.fori_loop(0, 9, row_pass, 0)

    x = 2.0 * lax.broadcasted_iota(jnp.int32, (1, CW), 1).astype(F32) / (CW - 1) - 1.0
    for n in range(CCDS):
        k = coef[n]
        wk[n, 0] = k[:, 0:1] + k[:, 1:2] * x + k[:, 3:4] * (x * x)
        wk[n, 1] = k[:, 2:3] + k[:, 4:5] * x
        wk[n, 2] = jnp.broadcast_to(k[:, 5:6], (27, CW))
    loads[5].wait()

    def column_ops(k, c):
        to = pl.ds(pl.multiple_of(k * CW, CW), CW)
        for n in range(CCDS):
            for p in range(3):
                m = jnp.zeros((CW, CW), F32)
                for b in range(3):
                    at = pl.ds(pl.multiple_of((k // 3 * 3 + b) * CW, CW), CW)
                    m = m + cop[at, :] * wk[n, p, pl.ds(3 * k + b, 1), :]
                high, low = split(m)
                m_hi[n, to, p * CW : (p + 1) * CW] = high
                m_lo[n, to, p * CW : (p + 1) * CW] = low
        return c

    lax.fori_loop(0, 9, column_ops, 0)
    y = 2.0 * lax.broadcasted_iota(jnp.int32, (CH, 1), 0).astype(F32) / (CH - 1) - 1.0
    for n in range(CCDS):
        o = dot(s_hi[n], m_hi[n]) + dot(s_hi[n], m_lo[n]) + dot(s_lo[n], m_hi[n])
        conv = o[:, :CW] + y * o[:, CW : 2 * CW] + (y * y) * o[:, 2 * CW :]
        at = pl.ds(n * CH, CH)
        use[at, :] = use[at, :] * conv

    roll_strips(use)
    for i in range(SR):
        high, low = split(tmp[pl.ds(i, STRIPS, stride=SR), :])
        fsend[pl.ds(i, DEVS * SLOTS, stride=SR), :] = dot(hot[...], high) + dot(hot[...], low)
    send_all(fsend, frecv, send_sem.at[2], fsem)

    own_meta.wait()
    all_meta = pltpu.make_async_remote_copy(
        src_ref=msend.at[pl.ds(0, DEVS - 1)],
        dst_ref=mrecv.at[pl.ds(0, DEVS - 1)],
        send_sem=send_sem.at[1],
        recv_sem=msem,
        device_id=(me, band),
        device_id_type=MESH,
    )
    all_meta.wait_recv()
    got = mrecv[...].reshape(DEVS, CW)
    totals = jnp.sum(got, axis=0, keepdims=True)
    weights = (totals + 1.0) / (pltpu.roll(totals, CW - 8, 1) + 1.0)
    lane_d = lax.broadcasted_iota(jnp.int32, (DEVS, CW), 1)
    for j in range(SLOTS):
        at = pl.ds(j * DEVS, DEVS)
        v = got[:, 8 * j + 2 : 8 * j + 3].astype(jnp.int32)
        vw = jnp.sum(
            jnp.where(lane_d == v + 16, jnp.broadcast_to(weights, (DEVS, CW)), 0.0),
            axis=1,
            keepdims=True,
        )
        rhs[at, 0:CW] = jnp.broadcast_to(got[:, 8 * j + 1 : 8 * j + 2], (DEVS, CW))
        rhs[at, CW : 2 * CW] = jnp.broadcast_to(got[:, 8 * j : 8 * j + 1], (DEVS, CW))
        rhs[at, 2 * CW :] = jnp.broadcast_to(vw, (DEVS, CW))
    spread_in = rhs[...].astype(BF16)
    weights_low = split(rhs[:, 2 * CW :])[1]

    k_sub = lax.broadcasted_iota(jnp.int32, (CHUNK, SLOTS * DEVS), 0)
    k_lane = lax.broadcasted_iota(jnp.int32, (CHUNK, SLOTS * DEVS), 1)
    lane_c = lax.broadcasted_iota(jnp.int32, (CHUNK, CW), 1).astype(F32)
    row_in = (lax.broadcasted_iota(jnp.int32, (CHUNK, CW), 0) % SR).astype(F32)

    def spread(p, c):
        at = pl.ds(pl.multiple_of(p * CHUNK, CHUNK), CHUNK)
        here = (k_lane - p * GROUP == k_sub // BLOCK + (k_sub // SR) % SLOTS * DEVS)
        here = here.astype(F32).astype(BF16)
        full = dot(here, spread_in)
        crep[at, :] = lane_c - (full[:, :CW] + COL_SHIFT)
        rt[at, :] = (lane_c == full[:, CW : 2 * CW] + row_in).astype(F32).astype(BF16)
        vrep[at, :] = full[:, 2 * CW :] + dot(here, weights_low)
        return c

    lax.fori_loop(0, PLANES, spread, 0)

    num[...] = jnp.zeros_like(num)
    wgt[...] = jnp.zeros_like(wgt)

    def place_all(src, recv, rsem, total):
        def one(p, c):
            at = pl.ds(pl.multiple_of(p * CHUNK, CHUNK), CHUNK)
            pltpu.make_async_copy(src.at[at], recv.at[at], rsem.at[p]).wait()
            high, low = split(recv[at, :] * vrep[at, :])
            off = crep[at, :]
            op = rt[at, :]
            zero = jnp.zeros_like(high)
            for t in range(PW // CW):
                away = off + float(t * CW)
                inside = (away >= 0.0) & (away < CW)
                cols = pl.ds(t * CW, CW)
                dims = (((0,), (0,)), ((), ()))
                total[:, cols] += lax.dot_general(
                    op, jnp.where(inside, high, zero), dims, preferred_element_type=F32
                ) + lax.dot_general(
                    op, jnp.where(inside, low, zero), dims, preferred_element_type=F32
                )
            return c

        lax.fori_loop(0, PLANES, one, 0)

    place_all(wsend, wrecv, wsem, wgt)
    place_all(fsend, frecv, fsem, num)
    wgt_o[...] = wgt[...]
    num_o[...] = num[...] / jnp.maximum(wgt[...], 1.0)

    all_meta.wait_send()
    for k, buf in ((0, wsend), (2, fsend)):
        rest = pl.ds(0, (DEVS - 1) * BLOCK)
        pltpu.make_async_copy(buf.at[rest], buf.at[rest], send_sem.at[k]).wait()


def shards(
    exposures, variance, mask_bits, kernel_coeffs, ccd_visit, strip_patch, strip_row, strip_col
):
    rhi, rlo, cop = tap_matrices()
    flat = (CCDS * CH, CW)
    anywhere = pl.BlockSpec(memory_space=pl.ANY)
    vmem = pl.BlockSpec(memory_space=pltpu.VMEM)
    smem = pl.BlockSpec(memory_space=pltpu.SMEM)
    slots = DEVS * BLOCK
    coadd, weight = pl.pallas_call(
        kernel,
        out_shape=[jax.ShapeDtypeStruct((PH, PW), F32)] * 2,
        in_specs=[anywhere] * 3 + [vmem, smem, vmem, vmem, vmem, smem] + [anywhere] * 3,
        out_specs=[vmem, vmem],
        scratch_shapes=[
            pltpu.VMEM(flat, jnp.int32),
            pltpu.VMEM(flat, F32),
            pltpu.VMEM(flat, F32),
            pltpu.VMEM(rhi.shape, BF16),
            pltpu.VMEM(rlo.shape, BF16),
            pltpu.VMEM(cop.shape, F32),
            pltpu.VMEM(flat, F32),
            pltpu.VMEM(flat, F32),
            pltpu.VMEM((CH, CCDS * CW), BF16),
            pltpu.VMEM((CH, CCDS * CW), BF16),
            pltpu.VMEM((CCDS, CH, 9 * CW), BF16),
            pltpu.VMEM((CCDS, CH, 9 * CW), BF16),
            pltpu.VMEM((CCDS, 9 * CW, 3 * CW), BF16),
            pltpu.VMEM((CCDS, 9 * CW, 3 * CW), BF16),
            pltpu.VMEM((CCDS, 3, 27, CW), F32),
            pltpu.VMEM((DEVS * SLOTS, STRIPS), BF16),
            pltpu.VMEM((slots, CW), F32),
            pltpu.VMEM((slots, CW), F32),
            pltpu.VMEM((DEVS, 1, CW), F32),
            pltpu.VMEM((slots, CW), F32),
            pltpu.VMEM((slots, CW), F32),
            pltpu.VMEM((DEVS, 1, CW), F32),
            pltpu.VMEM((slots, CW), F32),
            pltpu.VMEM((slots, CW), F32),
            pltpu.VMEM((slots, CW), BF16),
            pltpu.VMEM((SLOTS * DEVS, 3 * CW), F32),
            pltpu.VMEM((PH, PW), F32),
            pltpu.VMEM((PH, PW), F32),
            pltpu.SemaphoreType.DMA((7,)),
            pltpu.SemaphoreType.DMA((3,)),
            pltpu.SemaphoreType.DMA((PLANES,)),
            pltpu.SemaphoreType.DMA((PLANES,)),
            pltpu.SemaphoreType.DMA,
        ],
        compiler_params=pltpu.CompilerParams(
            collective_id=0, has_side_effects=True, vmem_limit_bytes=48 * 1024 * 1024
        ),
        cost_estimate=pl.CostEstimate(
            flops=2_600_000_000, bytes_accessed=6_000_000, transcendentals=0
        ),
    )(
        mask_bits.reshape(flat),
        variance.reshape(flat),
        exposures.reshape(flat),
        kernel_coeffs,
        ccd_visit,
        strip_patch.reshape(1, STRIPS),
        strip_row.reshape(1, STRIPS),
        strip_col.reshape(1, STRIPS),
        strip_col,
        jnp.asarray(rhi),
        jnp.asarray(rlo),
        jnp.asarray(cop),
    )
    return (coadd[None], weight[None])


def solution(mesh):
    return jax.shard_map(
        shards,
        mesh=mesh,
        in_specs=(
            P(("band", "patch"), None, None),
            P(("band", "patch"), None, None),
            P(("band", "patch"), None, None),
            P(("band", "patch"), None, None),
            P(("band", "patch"), None),
            P(("band", "patch"), None),
            P(("band", "patch")),
            P(("band", "patch")),
        ),
        out_specs=(P(("band", "patch"), None, None), P(("band", "patch"), None, None)),
        check_vma=False,
    )
```

```python
import functools

import jax
import jax.numpy as jnp
import numpy as np
from jax import lax
from jax.experimental import pallas as pl
from jax.experimental.pallas import tpu as pltpu
from jax.sharding import PartitionSpec as P

PH = 128
PW = 512
KS = 21
VISITS = 8
GAUSS_WIDTHS = (0.75, 1.5, 3.0)
MESH = pl.DeviceIdType.MESH
F32 = jnp.float32
BF16 = jnp.bfloat16

CCDS = 2
CH = 256
CW = 128
SR = 8
STRIPS = 64
DEVS = 64
NB = 27
SLOTS = 2
BLOCK = SLOTS * SR
PLANES = 8
GROUP = DEVS // PLANES
CHUNK = GROUP * BLOCK
COL_SHIFT = 192


def taps(offsets):
    half = KS // 2
    support = np.arange(-half, half + 1, dtype=np.float64)
    inside = np.abs(offsets) <= half
    tables = []
    for spread in GAUSS_WIDTHS:
        total = np.sum(np.exp(-support * support / (2.0 * spread * spread)))
        profile = np.where(inside, np.exp(-offsets * offsets / (2.0 * spread * spread)) / total, 0.0)
        scaled = offsets / spread
        tables += [profile, profile * scaled, profile * scaled * scaled]
    return np.stack(tables)


def tap_matrices():
    rows = np.arange(CH, dtype=np.float64)
    row_ops = taps(rows[None, :] - rows[:, None]).astype(np.float32).reshape(9 * CH, CH)
    cols = np.arange(CW, dtype=np.float64)
    col_ops = taps(cols[:, None] - cols[None, :]).astype(np.float32).reshape(9 * CW, CW)
    high = row_ops.astype(BF16)
    low = (row_ops - high.astype(np.float32)).astype(BF16)
    return high, low, col_ops


def split(x):
    high = x.astype(BF16)
    return high, (x - high.astype(F32)).astype(BF16)


def dot(a, b):
    return jnp.dot(a, b, preferred_element_type=F32)


def kernel(
    mask_h, var_h, exp_h, coef_h, visit_h, patch_h, row_h, col_h, rhi_h, rlo_h, cop_h,
    num_o, wgt_o,
    coef, visit_s, patch, row, col, col_s, mask, var, expo, rhi, rlo, cop, use, flux, tmp, e_hi, e_lo, s_hi, s_lo, m_hi, m_lo, wk,
    hot, wsend, fsend, msend, wrecv, frecv, mrecv, crep, vrep, rows_of, wide, rhs, num, wgt,
    load_sem, send_sem, wsem, fsem, msem,
):
    me = lax.axis_index("patch")
    band = lax.axis_index("band")
    my_plane = me // GROUP

    loads = [
        pltpu.make_async_copy(src, dst, load_sem.at[k])
        for k, (src, dst) in enumerate(
            [
                (patch_h, patch),
                (mask_h, mask),
                (col_h, col_s),
                (row_h, row),
                (col_h, col),
                (visit_h, visit_s),
                (var_h, var),
                (exp_h, expo),
                (coef_h, coef),
                (cop_h, cop),
                (rhi_h, rhi),
                (rlo_h, rlo),
            ]
        )
    ]
    for load in loads[:3]:
        load.start()

    barrier = pltpu.get_barrier_semaphore()

    def greet(k, c):
        pl.semaphore_signal(
            barrier, inc=1, device_id=(lax.rem(me + k, DEVS), band), device_id_type=MESH
        )
        return c

    lax.fori_loop(1, DEVS, greet, 0)
    for load in loads[3:]:
        load.start()

    loads[0].wait()
    lane = lax.broadcasted_iota(jnp.int32, (STRIPS, STRIPS), 1)
    sub = lax.broadcasted_iota(jnp.int32, (STRIPS, STRIPS), 0)
    prow = patch[...]
    pfull = jnp.broadcast_to(prow, (STRIPS, STRIPS))
    pcol = jnp.sum(jnp.where(lane == sub, pfull, 0), axis=1, keepdims=True)
    rank = jnp.sum(
        jnp.where((pcol == pfull) & (sub < lane), 1, 0), axis=0, keepdims=True
    )
    slot = prow * SLOTS + rank
    slot_id = lax.broadcasted_iota(jnp.int32, (DEVS * SLOTS, STRIPS), 0)
    hot[...] = (slot_id == slot).astype(F32).astype(BF16)

    def roll_strips(values):
        def one(s, c):
            at = pl.ds(pl.multiple_of(s * SR, SR), SR)
            tmp[at, :] = pltpu.roll(values[at, :], lax.bitwise_and(col_s[0, s], CW - 1), 1)
            return c

        lax.fori_loop(0, STRIPS, one, 0, unroll=8)

    loads[1].wait()
    loads[2].wait()
    use[...] = jnp.where(jnp.bitwise_and(mask[...], 3) != 3, 1.0, 0.0)
    roll_strips(use)
    for i in range(SR):
        wsend[pl.ds(i, DEVS * SLOTS, stride=SR), :] = dot(
            hot[...], tmp[pl.ds(i, STRIPS, stride=SR), :].astype(BF16)
        )

    def convolve():
        loads[7].wait()
        for c in range(CCDS):
            high, low = split(expo[c * CH : (c + 1) * CH, :])
            e_hi[:, c * CW : (c + 1) * CW] = high
            e_lo[:, c * CW : (c + 1) * CW] = low
        loads[10].wait()
        loads[11].wait()

        def row_pass(k, c):
            at = pl.ds(pl.multiple_of(k * CH, CH), CH)
            to = pl.ds(pl.multiple_of(k * CW, CW), CW)
            s = dot(rhi[at, :], e_hi[...]) + dot(rhi[at, :], e_lo[...]) + dot(rlo[at, :], e_hi[...])
            high, low = split(s)
            for n in range(CCDS):
                s_hi[n, :, to] = high[:, n * CW : (n + 1) * CW]
                s_lo[n, :, to] = low[:, n * CW : (n + 1) * CW]
            return c

        lax.fori_loop(0, 9, row_pass, 0)

        x = 2.0 * lax.broadcasted_iota(jnp.int32, (1, CW), 1).astype(F32) / (CW - 1) - 1.0
        loads[8].wait()
        basis = lax.broadcasted_iota(jnp.int32, (NB, NB), 0) == lax.broadcasted_iota(
            jnp.int32, (NB, NB), 1
        )

        def term(n, p):
            return jnp.sum(
                jnp.where(basis, jnp.broadcast_to(coef[p, n : n + 1, :], (NB, NB)), 0.0),
                axis=1,
                keepdims=True,
            )

        for n in range(CCDS):
            k = [term(n, p) for p in range(6)]
            wk[n, 0] = k[0] + k[1] * x + k[3] * (x * x)
            wk[n, 1] = k[2] + k[4] * x
            wk[n, 2] = jnp.broadcast_to(k[5], (NB, CW))
        loads[9].wait()

        def column_ops(k, c):
            to = pl.ds(pl.multiple_of(k * CW, CW), CW)
            for n in range(CCDS):
                for p in range(3):
                    m = jnp.zeros((CW, CW), F32)
                    for b in range(3):
                        at = pl.ds(pl.multiple_of((k // 3 * 3 + b) * CW, CW), CW)
                        m = m + cop[at, :] * wk[n, p, pl.ds(3 * k + b, 1), :]
                    high, low = split(m)
                    m_hi[n, to, p * CW : (p + 1) * CW] = high
                    m_lo[n, to, p * CW : (p + 1) * CW] = low
            return c

        lax.fori_loop(0, 9, column_ops, 0)
        y = 2.0 * lax.broadcasted_iota(jnp.int32, (CH, 1), 0).astype(F32) / (CH - 1) - 1.0
        for n in range(CCDS):
            o = dot(s_hi[n], m_hi[n]) + dot(s_hi[n], m_lo[n]) + dot(s_lo[n], m_hi[n])
            conv = o[:, :CW] + y * o[:, CW : 2 * CW] + (y * y) * o[:, 2 * CW :]
            at = pl.ds(n * CH, CH)
            flux[at, :] = use[at, :] * conv

    early = me < DEVS // 2

    @pl.when(early)
    def _():
        convolve()

    pl.semaphore_wait(barrier, DEVS - 1)

    def block(d):
        return pl.ds(pl.multiple_of(d * BLOCK, BLOCK), BLOCK)

    def each(half, act):
        def one(k, c):
            d = half * (DEVS // 2) + lax.rem(me + k, DEVS // 2)

            @pl.when(d != me)
            def _():
                act(d)

            return c

        lax.fori_loop(0, DEVS // 2, one, 0)

    def send_all(src, dst, ssem, rsem):
        def one(d):
            pltpu.make_async_remote_copy(
                src_ref=src.at[block(d)],
                dst_ref=dst.at[block(me)],
                send_sem=ssem,
                recv_sem=rsem.at[my_plane],
                device_id=(d, band),
                device_id_type=MESH,
            ).start()

        each(0, one)
        each(1, one)
        pltpu.make_async_copy(src.at[block(me)], dst.at[block(me)], rsem.at[my_plane]).start()

    send_all(wsend, wrecv, send_sem.at[0], wsem)

    for load in loads[3:7]:
        load.wait()
    lane1 = lax.broadcasted_iota(jnp.int32, (1, CW), 1)
    sums = jnp.zeros((1, CW), F32)
    for c in range(CCDS):
        u = use[c * CH : (c + 1) * CH, :]
        count = jnp.sum(u)
        amount = jnp.sum(u * var[c * CH : (c + 1) * CH, :])
        v = visit_s[0, c]
        sums = sums + jnp.where(lane1 == v + 16, count, 0.0) + jnp.where(lane1 == v + 24, amount, 0.0)
    strip_lane = lax.broadcasted_iota(jnp.int32, (1, STRIPS), 1)
    vrow = jnp.where(strip_lane < STRIPS // CCDS, visit_s[0, 0], visit_s[0, 1])
    q_sub = lax.broadcasted_iota(jnp.int32, (CW, STRIPS), 0)
    hot_id = lax.broadcasted_iota(jnp.int32, (DEVS, STRIPS), 0)
    meta = jnp.broadcast_to(sums, (DEVS, CW))
    for j in range(SLOTS):
        q = jnp.where(q_sub == 8 * j, row[...], 0)
        q = jnp.where(q_sub == 8 * j + 1, col[...] - COL_SHIFT, q)
        q = jnp.where(q_sub == 8 * j + 2, vrow, q)
        hot_j = (hot_id * SLOTS + j == slot).astype(F32).astype(BF16)
        meta = meta + lax.dot_general(
            hot_j, q.astype(F32).astype(BF16), (((1,), (1,)), ((), ())), preferred_element_type=F32
        )
    msend[...] = meta.reshape(DEVS, 1, CW)

    def send_meta(k, c):
        d = lax.rem(me + k, DEVS)
        pltpu.make_async_remote_copy(
            src_ref=msend.at[d],
            dst_ref=mrecv.at[me],
            send_sem=send_sem.at[1],
            recv_sem=msem,
            device_id=(d, band),
            device_id_type=MESH,
        ).start()
        return c

    lax.fori_loop(1, DEVS, send_meta, 0)
    own_meta = pltpu.make_async_copy(msend.at[me], mrecv.at[me], load_sem.at[12])
    own_meta.start()

    @pl.when(jnp.logical_not(early))
    def _():
        convolve()

    roll_strips(flux)
    for i in range(SR):
        high, low = split(tmp[pl.ds(i, STRIPS, stride=SR), :])
        fsend[pl.ds(i, DEVS * SLOTS, stride=SR), :] = dot(hot[...], high) + dot(hot[...], low)
    send_all(fsend, frecv, send_sem.at[2], fsem)

    own_meta.wait()
    all_meta = pltpu.make_async_remote_copy(
        src_ref=msend.at[pl.ds(0, DEVS - 1)],
        dst_ref=mrecv.at[pl.ds(0, DEVS - 1)],
        send_sem=send_sem.at[1],
        recv_sem=msem,
        device_id=(me, band),
        device_id_type=MESH,
    )
    all_meta.wait_recv()
    got = mrecv[...].reshape(DEVS, CW)
    totals = jnp.sum(got, axis=0, keepdims=True)
    weights = (totals + 1.0) / (pltpu.roll(totals, CW - 8, 1) + 1.0)
    lane_d = lax.broadcasted_iota(jnp.int32, (DEVS, CW), 1)
    for j in range(SLOTS):
        at = pl.ds(j * DEVS, DEVS)
        v = got[:, 8 * j + 2 : 8 * j + 3].astype(jnp.int32)
        vw = jnp.sum(
            jnp.where(lane_d == v + 16, jnp.broadcast_to(weights, (DEVS, CW)), 0.0),
            axis=1,
            keepdims=True,
        )
        rhs[at, 0:CW] = jnp.broadcast_to(got[:, 8 * j + 1 : 8 * j + 2], (DEVS, CW))
        rhs[at, CW : 2 * CW] = jnp.broadcast_to(got[:, 8 * j : 8 * j + 1], (DEVS, CW))
        rhs[at, 2 * CW :] = jnp.broadcast_to(vw, (DEVS, CW))
    spread_in = rhs[...].astype(BF16)
    weights_low = split(rhs[:, 2 * CW :])[1]

    k_sub = lax.broadcasted_iota(jnp.int32, (CHUNK, SLOTS * DEVS), 0)
    k_lane = lax.broadcasted_iota(jnp.int32, (CHUNK, SLOTS * DEVS), 1)
    lane_c = lax.broadcasted_iota(jnp.int32, (CHUNK, CW), 1).astype(F32)
    row_in = (lax.broadcasted_iota(jnp.int32, (CHUNK, CW), 0) % SR).astype(F32)

    def spread(p, c):
        at = pl.ds(pl.multiple_of(p * CHUNK, CHUNK), CHUNK)
        here = (k_lane - p * GROUP == k_sub // BLOCK + (k_sub // SR) % SLOTS * DEVS)
        here = here.astype(F32).astype(BF16)
        full = dot(here, spread_in)
        crep[at, :] = lane_c - (full[:, :CW] + COL_SHIFT)
        rt = (lane_c == full[:, CW : 2 * CW] + row_in).astype(F32)
        turned = jnp.transpose(rt).astype(BF16)
        rows_of[p, :, 0:CHUNK] = turned
        rows_of[p, :, CHUNK : 2 * CHUNK] = turned
        vrep[at, :] = full[:, 2 * CW :] + dot(here, weights_low)
        return c

    lax.fori_loop(0, PLANES, spread, 0)

    num[...] = jnp.zeros_like(num)
    wgt[...] = jnp.zeros_like(wgt)

    def place_all(src, recv, rsem, total):
        def one(p, c):
            at = pl.ds(pl.multiple_of(p * CHUNK, CHUNK), CHUNK)
            pltpu.make_async_copy(src.at[at], recv.at[at], rsem.at[p]).wait()
            high, low = split(recv[at, :] * vrep[at, :])
            off = crep[at, :]
            zero = jnp.zeros_like(high)
            for t in range(PW // CW):
                away = off + float(t * CW)
                inside = (away >= 0.0) & (away < CW)
                cols = pl.ds(t * CW, CW)
                wide[0:CHUNK, cols] = jnp.where(inside, high, zero)
                wide[CHUNK : 2 * CHUNK, cols] = jnp.where(inside, low, zero)
            total[...] += dot(rows_of[p], wide[...])
            return c

        lax.fori_loop(0, PLANES, one, 0)

    place_all(wsend, wrecv, wsem, wgt)
    place_all(fsend, frecv, fsem, num)
    wgt_o[...] = wgt[...]
    num_o[...] = num[...]

    all_meta.wait_send()
    for k, buf in ((0, wsend), (2, fsend)):
        rest = pl.ds(0, (DEVS - 1) * BLOCK)
        pltpu.make_async_copy(buf.at[rest], buf.at[rest], send_sem.at[k]).wait()


def shards(
    exposures, variance, mask_bits, kernel_coeffs, ccd_visit, strip_patch, strip_row, strip_col
):
    rhi, rlo, cop = tap_matrices()
    flat = (CCDS * CH, CW)
    hbm = pl.BlockSpec(memory_space=pltpu.HBM)
    vmem = pl.BlockSpec(memory_space=pltpu.VMEM)
    slots = DEVS * BLOCK
    num, wgt = pl.pallas_call(
        kernel,
        out_shape=[jax.ShapeDtypeStruct((PH, PW), F32)] * 2,
        in_specs=[hbm] * 11,
        out_specs=[vmem, vmem],
        scratch_shapes=[
            pltpu.VMEM((6, CCDS, NB), F32),
            pltpu.SMEM((1, CCDS), jnp.int32),
            pltpu.VMEM((1, STRIPS), jnp.int32),
            pltpu.VMEM((1, STRIPS), jnp.int32),
            pltpu.VMEM((1, STRIPS), jnp.int32),
            pltpu.SMEM((1, STRIPS), jnp.int32),
            pltpu.VMEM(flat, jnp.int32),
            pltpu.VMEM(flat, F32),
            pltpu.VMEM(flat, F32),
            pltpu.VMEM(rhi.shape, BF16),
            pltpu.VMEM(rlo.shape, BF16),
            pltpu.VMEM(cop.shape, F32),
            pltpu.VMEM(flat, F32),
            pltpu.VMEM(flat, F32),
            pltpu.VMEM(flat, F32),
            pltpu.VMEM((CH, CCDS * CW), BF16),
            pltpu.VMEM((CH, CCDS * CW), BF16),
            pltpu.VMEM((CCDS, CH, 9 * CW), BF16),
            pltpu.VMEM((CCDS, CH, 9 * CW), BF16),
            pltpu.VMEM((CCDS, 9 * CW, 3 * CW), BF16),
            pltpu.VMEM((CCDS, 9 * CW, 3 * CW), BF16),
            pltpu.VMEM((CCDS, 3, NB, CW), F32),
            pltpu.VMEM((DEVS * SLOTS, STRIPS), BF16),
            pltpu.VMEM((slots, CW), F32),
            pltpu.VMEM((slots, CW), F32),
            pltpu.VMEM((DEVS, 1, CW), F32),
            pltpu.VMEM((slots, CW), F32),
            pltpu.VMEM((slots, CW), F32),
            pltpu.VMEM((DEVS, 1, CW), F32),
            pltpu.VMEM((slots, CW), F32),
            pltpu.VMEM((slots, CW), F32),
            pltpu.VMEM((PLANES, PH, 2 * CHUNK), BF16),
            pltpu.VMEM((2 * CHUNK, PW), BF16),
            pltpu.VMEM((SLOTS * DEVS, 3 * CW), F32),
            pltpu.VMEM((PH, PW), F32),
            pltpu.VMEM((PH, PW), F32),
            pltpu.SemaphoreType.DMA((13,)),
            pltpu.SemaphoreType.DMA((3,)),
            pltpu.SemaphoreType.DMA((PLANES,)),
            pltpu.SemaphoreType.DMA((PLANES,)),
            pltpu.SemaphoreType.DMA,
        ],
        compiler_params=pltpu.CompilerParams(
            collective_id=0, has_side_effects=True, vmem_limit_bytes=40 * 1024 * 1024
        ),
        cost_estimate=pl.CostEstimate(
            flops=2_600_000_000, bytes_accessed=6_000_000, transcendentals=0
        ),
    )(
        *(
            pltpu.with_memory_space_constraint(operand, pltpu.HBM)
            for operand in (
                mask_bits.reshape(flat),
                variance.reshape(flat),
                exposures.reshape(flat),
                kernel_coeffs.transpose(2, 0, 1),
                ccd_visit.reshape(1, CCDS),
                strip_patch.reshape(1, STRIPS),
                strip_row.reshape(1, STRIPS),
                strip_col.reshape(1, STRIPS),
                jnp.asarray(rhi),
                jnp.asarray(rlo),
                jnp.asarray(cop),
            )
        )
    )
    return ((num / jnp.maximum(wgt, 1.0))[None], jnp.maximum(wgt, 0.0)[None])


def solution(mesh):
    return jax.shard_map(
        shards,
        mesh=mesh,
        in_specs=(
            P(("band", "patch"), None, None),
            P(("band", "patch"), None, None),
            P(("band", "patch"), None, None),
            P(("band", "patch"), None, None),
            P(("band", "patch"), None),
            P(("band", "patch"), None),
            P(("band", "patch")),
            P(("band", "patch")),
        ),
        out_specs=(P(("band", "patch"), None, None), P(("band", "patch"), None, None)),
        check_vma=False,
    )
```

```python
import functools

import jax
import jax.numpy as jnp
import numpy as np
from jax import lax
from jax.experimental import pallas as pl
from jax.experimental.pallas import tpu as pltpu
from jax.sharding import PartitionSpec as P

PH = 128
PW = 512
KS = 21
VISITS = 8
GAUSS_WIDTHS = (0.75, 1.5, 3.0)
MESH = pl.DeviceIdType.MESH
F32 = jnp.float32
BF16 = jnp.bfloat16

CCDS = 2
CH = 256
CW = 128
SR = 8
STRIPS = 64
DEVS = 64
NB = 27
SLOTS = 2
BLOCK = SLOTS * SR
PLANES = 8
GROUP = DEVS // PLANES
BANDS = 4
FLUX_ONLY = ("exposures", "row_high", "row_low", "coefficients", "column_taps")
CHUNK = GROUP * BLOCK
COL_SHIFT = 192


def taps(offsets):
    half = KS // 2
    support = np.arange(-half, half + 1, dtype=np.float64)
    inside = np.abs(offsets) <= half
    tables = []
    for spread in GAUSS_WIDTHS:
        total = np.sum(np.exp(-support * support / (2.0 * spread * spread)))
        profile = np.where(inside, np.exp(-offsets * offsets / (2.0 * spread * spread)) / total, 0.0)
        scaled = offsets / spread
        tables += [profile, profile * scaled, profile * scaled * scaled]
    return np.stack(tables)


def tap_matrices():
    rows = np.arange(CH, dtype=np.float64)
    row_ops = taps(rows[None, :] - rows[:, None]).astype(np.float32).reshape(9 * CH, CH)
    cols = np.arange(CW, dtype=np.float64)
    col_ops = taps(cols[:, None] - cols[None, :]).astype(np.float32).reshape(9 * CW, CW)
    high = row_ops.astype(BF16)
    low = (row_ops - high.astype(np.float32)).astype(BF16)
    return high, low, col_ops


def split(x):
    high = x.astype(BF16)
    return high, (x - high.astype(F32)).astype(BF16)


def dot(a, b):
    return jnp.dot(a, b, preferred_element_type=F32)


def kernel(
    flux_mode,
    mask_h, var_h, exp_h, coef_h, visit_h, patch_h, row_h, col_h, rhi_h, rlo_h, cop_h,
    *refs,
):
    if flux_mode:
        num_o, wgt_o, flag_o, *refs = refs
    else:
        wgt_o, *refs = refs
    (
        coef, visit_s, patch, row, col, col_s, mask, var, expo, rhi, rlo, cop,
        use, tmp, e_hi, e_lo, s_hi, s_lo, m_hi, m_lo, wk,
        hot, packed, msend, arrived, mrecv, crep, vrep, rows_of, wide, rhs, placed,
        flag_out, flag_plane, flag_z, flag_band,
        load_sem, send_sem, data_sem, msem, flag_sem,
    ) = refs
    me = lax.axis_index("patch")
    band = lax.axis_index("band")
    my_plane = me // GROUP

    loads = {
        name: pltpu.make_async_copy(src, dst, load_sem.at[k])
        for k, (name, src, dst) in enumerate(
            [
                ("exposures", exp_h, expo),
                ("row_high", rhi_h, rhi),
                ("row_low", rlo_h, rlo),
                ("mask", mask_h, mask),
                ("patch", patch_h, patch),
                ("col_scalar", col_h, col_s),
                ("row", row_h, row),
                ("col", col_h, col),
                ("visit", visit_h, visit_s),
                ("variance", var_h, var),
                ("coefficients", coef_h, coef),
                ("column_taps", cop_h, cop),
            ]
        )
        if flux_mode or name not in FLUX_ONLY
    }
    for load in loads.values():
        load.start()

    barrier = pltpu.get_barrier_semaphore()

    def greet(k, c):
        pl.semaphore_signal(
            barrier, inc=1, device_id=(lax.rem(me + k, DEVS), band), device_id_type=MESH
        )
        return c

    lax.fori_loop(1, DEVS, greet, 0)
    if flux_mode:
        for k in range(1, BANDS):
            pl.semaphore_signal(
                barrier, inc=1, device_id=(me, lax.rem(band + k, BANDS)), device_id_type=MESH
            )
    greeted = DEVS - 1 + (BANDS - 1 if flux_mode else 0)

    if flux_mode:
        loads["exposures"].wait()
        for c in range(CCDS):
            high, low = split(expo[c * CH : (c + 1) * CH, :])
            e_hi[:, c * CW : (c + 1) * CW] = high
            e_lo[:, c * CW : (c + 1) * CW] = low
        loads["row_high"].wait()
        loads["row_low"].wait()

        def row_pass(k, c):
            at = pl.ds(pl.multiple_of(k * CH, CH), CH)
            to = pl.ds(pl.multiple_of(k * CW, CW), CW)
            s = dot(rhi[at, :], e_hi[...]) + dot(rhi[at, :], e_lo[...]) + dot(rlo[at, :], e_hi[...])
            high, low = split(s)
            for n in range(CCDS):
                s_hi[n, :, to] = high[:, n * CW : (n + 1) * CW]
                s_lo[n, :, to] = low[:, n * CW : (n + 1) * CW]
            return c

        lax.fori_loop(0, 9, row_pass, 0)

    loads["patch"].wait()
    lane = lax.broadcasted_iota(jnp.int32, (STRIPS, STRIPS), 1)
    sub = lax.broadcasted_iota(jnp.int32, (STRIPS, STRIPS), 0)
    prow = patch[...]
    pfull = jnp.broadcast_to(prow, (STRIPS, STRIPS))
    pcol = jnp.sum(jnp.where(lane == sub, pfull, 0), axis=1, keepdims=True)
    rank = jnp.sum(
        jnp.where((pcol == pfull) & (sub < lane), 1, 0), axis=0, keepdims=True
    )
    slot = prow * SLOTS + rank
    slot_id = lax.broadcasted_iota(jnp.int32, (DEVS * SLOTS, STRIPS), 0)
    hot[...] = (slot_id == slot).astype(F32).astype(BF16)

    loads["mask"].wait()
    use[...] = jnp.where(jnp.bitwise_and(mask[...], 3) != 3, 1.0, 0.0)
    for name in ("row", "col", "col_scalar", "visit", "variance"):
        loads[name].wait()
    lane1 = lax.broadcasted_iota(jnp.int32, (1, CW), 1)
    sums = jnp.zeros((1, CW), F32)
    usable_count = 0.0
    for c in range(CCDS):
        u = use[c * CH : (c + 1) * CH, :]
        count = jnp.sum(u)
        amount = jnp.sum(u * var[c * CH : (c + 1) * CH, :])
        usable_count = usable_count + count
        v = visit_s[0, c]
        sums = sums + jnp.where(lane1 == v + 16, count, 0.0) + jnp.where(lane1 == v + 24, amount, 0.0)
    strip_lane = lax.broadcasted_iota(jnp.int32, (1, STRIPS), 1)
    vrow = jnp.where(strip_lane < STRIPS // CCDS, visit_s[0, 0], visit_s[0, 1])
    q_sub = lax.broadcasted_iota(jnp.int32, (CW, STRIPS), 0)
    hot_id = lax.broadcasted_iota(jnp.int32, (DEVS, STRIPS), 0)
    meta = jnp.broadcast_to(sums, (DEVS, CW))
    for j in range(SLOTS):
        q = jnp.where(q_sub == 8 * j, row[...], 0)
        q = jnp.where(q_sub == 8 * j + 1, col[...] - COL_SHIFT, q)
        q = jnp.where(q_sub == 8 * j + 2, vrow, q)
        hot_j = (hot_id * SLOTS + j == slot).astype(F32).astype(BF16)
        meta = meta + lax.dot_general(
            hot_j, q.astype(F32).astype(BF16), (((1,), (1,)), ((), ())), preferred_element_type=F32
        )
    msend[...] = meta.reshape(DEVS, 1, CW)

    pl.semaphore_wait(barrier, greeted)

    def send_meta(k):
        d = lax.rem(me + k, DEVS)
        pltpu.make_async_remote_copy(
            src_ref=msend.at[d],
            dst_ref=mrecv.at[me],
            send_sem=send_sem.at[1],
            recv_sem=msem,
            device_id=(d, band),
            device_id_type=MESH,
        ).start()

    own_meta = pltpu.make_async_copy(msend.at[me], mrecv.at[me], load_sem.at[12])
    own_meta.start()

    if flux_mode:
        x = 2.0 * lax.broadcasted_iota(jnp.int32, (1, CW), 1).astype(F32) / (CW - 1) - 1.0
        loads["coefficients"].wait()
        basis = lax.broadcasted_iota(jnp.int32, (NB, NB), 0) == lax.broadcasted_iota(
            jnp.int32, (NB, NB), 1
        )

        def term(n, p):
            return jnp.sum(
                jnp.where(basis, jnp.broadcast_to(coef[p, n : n + 1, :], (NB, NB)), 0.0),
                axis=1,
                keepdims=True,
            )

        for n in range(CCDS):
            k = [term(n, p) for p in range(6)]
            wk[n, 0] = k[0] + k[1] * x + k[3] * (x * x)
            wk[n, 1] = k[2] + k[4] * x
            wk[n, 2] = jnp.broadcast_to(k[5], (NB, CW))
        loads["column_taps"].wait()

        def column_ops(k, c):
            for q in range(7):
                send_meta(7 * k + q + 1)
            to = pl.ds(pl.multiple_of(k * CW, CW), CW)
            for n in range(CCDS):
                for p in range(3):
                    m = jnp.zeros((CW, CW), F32)
                    for b in range(3):
                        at = pl.ds(pl.multiple_of((k // 3 * 3 + b) * CW, CW), CW)
                        m = m + cop[at, :] * wk[n, p, pl.ds(3 * k + b, 1), :]
                    high, low = split(m)
                    m_hi[n, to, p * CW : (p + 1) * CW] = high
                    m_lo[n, to, p * CW : (p + 1) * CW] = low
            return c

        lax.fori_loop(0, 9, column_ops, 0)
        y = 2.0 * lax.broadcasted_iota(jnp.int32, (CH, 1), 0).astype(F32) / (CH - 1) - 1.0
        for n in range(CCDS):
            o = dot(s_hi[n], m_hi[n]) + dot(s_hi[n], m_lo[n]) + dot(s_lo[n], m_hi[n])
            conv = o[:, :CW] + y * o[:, CW : 2 * CW] + (y * y) * o[:, 2 * CW :]
            at = pl.ds(n * CH, CH)
            use[at, :] = use[at, :] * conv
    else:

        def meta_step(k, c):
            send_meta(k)
            return c

        lax.fori_loop(1, DEVS, meta_step, 0)

    def roll_strip(s, c):
        at = pl.ds(pl.multiple_of(s * SR, SR), SR)
        tmp[at, :] = pltpu.roll(use[at, :], lax.bitwise_and(col_s[0, s], CW - 1), 1)
        return c

    lax.fori_loop(0, STRIPS, roll_strip, 0, unroll=8)
    for i in range(SR):
        high, low = split(tmp[pl.ds(i, STRIPS, stride=SR), :])
        packed[pl.ds(i, DEVS * SLOTS, stride=SR), :] = dot(hot[...], high) + dot(hot[...], low)

    def block(d):
        return pl.ds(pl.multiple_of(d * BLOCK, BLOCK), BLOCK)

    def send_half(half):
        def one(k, c):
            d = half * (DEVS // 2) + lax.rem(me + k, DEVS // 2)

            @pl.when(d != me)
            def _():
                pltpu.make_async_remote_copy(
                    src_ref=packed.at[block(d)],
                    dst_ref=arrived.at[block(me)],
                    send_sem=send_sem.at[0],
                    recv_sem=data_sem.at[my_plane],
                    device_id=(d, band),
                    device_id_type=MESH,
                ).start()

            return c

        lax.fori_loop(0, DEVS // 2, one, 0)

    send_half(0)
    send_half(1)
    pltpu.make_async_copy(
        packed.at[block(me)], arrived.at[block(me)], data_sem.at[my_plane]
    ).start()

    def flag_round(r, value, land, mine, peers):
        flag_out[r] = value
        land[mine] = value
        for device_id in peers:
            pltpu.make_async_remote_copy(
                src_ref=flag_out.at[r],
                dst_ref=land.at[mine],
                send_sem=flag_sem.at[0, r],
                recv_sem=flag_sem.at[1, r],
                device_id=device_id,
                device_id_type=MESH,
            ).start()

    def flag_end(r, land):
        n = land.shape[0] - 1
        for k in range(2):
            rest = land.at[pl.ds(0, n)]
            pltpu.make_async_copy(rest, rest, flag_sem.at[k, r]).wait()
        return jnp.max(land[...].reshape(n + 1, CW), axis=0, keepdims=True)

    mine = lax.rem(me, GROUP)
    if flux_mode:
        nonzero = jnp.sum(jnp.where(packed[...] != 0.0, 1.0, 0.0))
        flag = jnp.zeros((1, CW), F32) + (usable_count - nonzero)
        flag_round(
            0, flag, flag_plane, mine,
            [(my_plane * GROUP + lax.rem(mine + k, GROUP), band) for k in range(1, GROUP)],
        )

    own_meta.wait()
    all_meta = pltpu.make_async_remote_copy(
        src_ref=msend.at[pl.ds(0, DEVS - 1)],
        dst_ref=mrecv.at[pl.ds(0, DEVS - 1)],
        send_sem=send_sem.at[1],
        recv_sem=msem,
        device_id=(me, band),
        device_id_type=MESH,
    )
    all_meta.wait_recv()
    if flux_mode:
        flag_round(
            1, flag_end(0, flag_plane), flag_z, my_plane,
            [(lax.rem(me + k * GROUP, DEVS), band) for k in range(1, PLANES)],
        )
    got = mrecv[...].reshape(DEVS, CW)
    totals = jnp.sum(got, axis=0, keepdims=True)
    weights = (totals + 1.0) / (pltpu.roll(totals, CW - 8, 1) + 1.0)
    lane_d = lax.broadcasted_iota(jnp.int32, (DEVS, CW), 1)
    for j in range(SLOTS):
        at = pl.ds(j * DEVS, DEVS)
        v = got[:, 8 * j + 2 : 8 * j + 3].astype(jnp.int32)
        vw = jnp.sum(
            jnp.where(lane_d == v + 16, jnp.broadcast_to(weights, (DEVS, CW)), 0.0),
            axis=1,
            keepdims=True,
        )
        rhs[at, 0:CW] = jnp.broadcast_to(got[:, 8 * j + 1 : 8 * j + 2], (DEVS, CW))
        rhs[at, CW : 2 * CW] = jnp.broadcast_to(got[:, 8 * j : 8 * j + 1], (DEVS, CW))
        rhs[at, 2 * CW :] = jnp.broadcast_to(vw, (DEVS, CW))
    spread_in = rhs[...].astype(BF16)
    weights_low = split(rhs[:, 2 * CW :])[1]

    k_sub = lax.broadcasted_iota(jnp.int32, (CHUNK, SLOTS * DEVS), 0)
    k_lane = lax.broadcasted_iota(jnp.int32, (CHUNK, SLOTS * DEVS), 1)
    lane_c = lax.broadcasted_iota(jnp.int32, (CHUNK, CW), 1).astype(F32)
    row_in = (lax.broadcasted_iota(jnp.int32, (CHUNK, CW), 0) % SR).astype(F32)

    def spread(p, c):
        at = pl.ds(pl.multiple_of(p * CHUNK, CHUNK), CHUNK)
        here = (k_lane - p * GROUP == k_sub // BLOCK + (k_sub // SR) % SLOTS * DEVS)
        here = here.astype(F32).astype(BF16)
        full = dot(here, spread_in)
        crep[at, :] = lane_c - (full[:, :CW] + COL_SHIFT)
        rt = (lane_c == full[:, CW : 2 * CW] + row_in).astype(F32)
        turned = jnp.transpose(rt).astype(BF16)
        rows_of[p, :, 0:CHUNK] = turned
        rows_of[p, :, CHUNK : 2 * CHUNK] = turned
        vrep[at, :] = full[:, 2 * CW :] + dot(here, weights_low)
        return c

    lax.fori_loop(0, PLANES, spread, 0)
    if flux_mode:
        flag_round(
            2, flag_end(1, flag_z), flag_band, band,
            [(me, lax.rem(band + k, BANDS)) for k in range(1, BANDS)],
        )

    placed[...] = jnp.zeros_like(placed)

    def place(p, c):
        at = pl.ds(pl.multiple_of(p * CHUNK, CHUNK), CHUNK)
        pltpu.make_async_copy(packed.at[at], arrived.at[at], data_sem.at[p]).wait()
        value = arrived[at, :]
        weight = vrep[at, :]
        maps = [value * weight]
        if flux_mode:
            maps.append(jnp.where(value != 0.0, weight, 0.0))
        off = crep[at, :]
        for n, (high, low) in enumerate(split(m) for m in maps):
            zero = jnp.zeros_like(high)
            for t in range(PW // CW):
                away = off + float(t * CW)
                inside = (away >= 0.0) & (away < CW)
                cols = pl.ds(n * PW + t * CW, CW)
                wide[0:CHUNK, cols] = jnp.where(inside, high, zero)
                wide[CHUNK : 2 * CHUNK, cols] = jnp.where(inside, low, zero)
        placed[...] += dot(rows_of[p], wide[...])
        return c

    lax.fori_loop(0, PLANES, place, 0)
    if flux_mode:
        num_o[...] = placed[:, :PW]
        wgt_o[...] = placed[:, PW:]
        flag_o[...] = flag_end(2, flag_band)
    else:
        wgt_o[...] = placed[...]

    all_meta.wait_send()
    rest = packed.at[pl.ds(0, (DEVS - 1) * BLOCK)]
    pltpu.make_async_copy(rest, rest, send_sem.at[0]).wait()


def exchange(flux_mode, operands):
    slots = DEVS * BLOCK
    flat = (CCDS * CH, CW)
    hbm = pl.BlockSpec(memory_space=pltpu.HBM)
    vmem = pl.BlockSpec(memory_space=pltpu.VMEM)
    image = jax.ShapeDtypeStruct((PH, PW), F32)
    outs = [image, image, jax.ShapeDtypeStruct((1, CW), F32)] if flux_mode else [image]
    maps = 2 if flux_mode else 1
    return pl.pallas_call(
        functools.partial(kernel, flux_mode),
        out_shape=outs,
        in_specs=[hbm] * 11,
        out_specs=[vmem] * len(outs),
        scratch_shapes=[
            pltpu.VMEM((6, CCDS, NB), F32),
            pltpu.SMEM((1, CCDS), jnp.int32),
            pltpu.VMEM((1, STRIPS), jnp.int32),
            pltpu.VMEM((1, STRIPS), jnp.int32),
            pltpu.VMEM((1, STRIPS), jnp.int32),
            pltpu.SMEM((1, STRIPS), jnp.int32),
            pltpu.VMEM(flat, jnp.int32),
            pltpu.VMEM(flat, F32),
            pltpu.VMEM(flat, F32),
            pltpu.VMEM((9 * CH, CH), BF16),
            pltpu.VMEM((9 * CH, CH), BF16),
            pltpu.VMEM((9 * CW, CW), F32),
            pltpu.VMEM(flat, F32),
            pltpu.VMEM(flat, F32),
            pltpu.VMEM((CH, CCDS * CW), BF16),
            pltpu.VMEM((CH, CCDS * CW), BF16),
            pltpu.VMEM((CCDS, CH, 9 * CW), BF16),
            pltpu.VMEM((CCDS, CH, 9 * CW), BF16),
            pltpu.VMEM((CCDS, 9 * CW, 3 * CW), BF16),
            pltpu.VMEM((CCDS, 9 * CW, 3 * CW), BF16),
            pltpu.VMEM((CCDS, 3, NB, CW), F32),
            pltpu.VMEM((DEVS * SLOTS, STRIPS), BF16),
            pltpu.VMEM((slots, CW), F32),
            pltpu.VMEM((DEVS, 1, CW), F32),
            pltpu.VMEM((slots, CW), F32),
            pltpu.VMEM((DEVS, 1, CW), F32),
            pltpu.VMEM((slots, CW), F32),
            pltpu.VMEM((slots, CW), F32),
            pltpu.VMEM((PLANES, PH, 2 * CHUNK), BF16),
            pltpu.VMEM((2 * CHUNK, maps * PW), BF16),
            pltpu.VMEM((SLOTS * DEVS, 3 * CW), F32),
            pltpu.VMEM((PH, maps * PW), F32),
            pltpu.VMEM((3, 1, CW), F32),
            pltpu.VMEM((GROUP, 1, CW), F32),
            pltpu.VMEM((PLANES, 1, CW), F32),
            pltpu.VMEM((BANDS, 1, CW), F32),
            pltpu.SemaphoreType.DMA((13,)),
            pltpu.SemaphoreType.DMA((2,)),
            pltpu.SemaphoreType.DMA((PLANES,)),
            pltpu.SemaphoreType.DMA,
            pltpu.SemaphoreType.DMA((2, 3)),
        ],
        compiler_params=pltpu.CompilerParams(
            collective_id=0 if flux_mode else 1,
            has_side_effects=True,
            vmem_limit_bytes=40 * 1024 * 1024,
        ),
        cost_estimate=pl.CostEstimate(
            flops=2_600_000_000, bytes_accessed=6_000_000, transcendentals=0
        ),
    )(*(pltpu.with_memory_space_constraint(operand, pltpu.HBM) for operand in operands))


def shards(
    exposures, variance, mask_bits, kernel_coeffs, ccd_visit, strip_patch, strip_row, strip_col
):
    rhi, rlo, cop = tap_matrices()
    flat = (CCDS * CH, CW)
    operands = (
        mask_bits.reshape(flat),
        variance.reshape(flat),
        exposures.reshape(flat),
        kernel_coeffs.transpose(2, 0, 1),
        ccd_visit.reshape(1, CCDS),
        strip_patch.reshape(1, STRIPS),
        strip_row.reshape(1, STRIPS),
        strip_col.reshape(1, STRIPS),
        jnp.asarray(rhi),
        jnp.asarray(rlo),
        jnp.asarray(cop),
    )
    num, wgt, flag = exchange(True, operands)

    def finish(num, wgt):
        return (num / jnp.maximum(wgt, 1.0))[None], jnp.maximum(wgt, 0.0)[None]

    return lax.cond(
        flag[0, 0] > 0.0,
        lambda: finish(num, exchange(False, operands)[0]),
        lambda: finish(num, wgt),
    )


def solution(mesh):
    return jax.shard_map(
        shards,
        mesh=mesh,
        in_specs=(
            P(("band", "patch"), None, None),
            P(("band", "patch"), None, None),
            P(("band", "patch"), None, None),
            P(("band", "patch"), None, None),
            P(("band", "patch"), None),
            P(("band", "patch"), None),
            P(("band", "patch")),
            P(("band", "patch")),
        ),
        out_specs=(P(("band", "patch"), None, None), P(("band", "patch"), None, None)),
        check_vma=False,
    )
```

```python
import functools

import jax
import jax.numpy as jnp
import numpy as np
from jax import lax
from jax.experimental import pallas as pl
from jax.experimental.pallas import tpu as pltpu
from jax.sharding import PartitionSpec as P

PH = 128
PW = 512
KS = 21
VISITS = 8
GAUSS_WIDTHS = (0.75, 1.5, 3.0)
MESH = pl.DeviceIdType.MESH
F32 = jnp.float32
BF16 = jnp.bfloat16

CCDS = 2
CH = 256
CW = 128
SR = 8
STRIPS = 64
DEVS = 64
NB = 27
SLOTS = 2
BLOCK = SLOTS * SR
PLANES = 8
GROUP = DEVS // PLANES
BANDS = 4
FLUX_ONLY = ("exposures", "row_high", "row_low", "coefficients", "column_taps")
CHUNK = GROUP * BLOCK
COL_SHIFT = 192


def taps(offsets):
    half = KS // 2
    support = np.arange(-half, half + 1, dtype=np.float64)
    inside = np.abs(offsets) <= half
    tables = []
    for spread in GAUSS_WIDTHS:
        total = np.sum(np.exp(-support * support / (2.0 * spread * spread)))
        profile = np.where(inside, np.exp(-offsets * offsets / (2.0 * spread * spread)) / total, 0.0)
        scaled = offsets / spread
        tables += [profile, profile * scaled, profile * scaled * scaled]
    return np.stack(tables)


def tap_matrices():
    rows = np.arange(CH, dtype=np.float64)
    row_ops = taps(rows[None, :] - rows[:, None]).astype(np.float32).reshape(9 * CH, CH)
    cols = np.arange(CW, dtype=np.float64)
    col_ops = taps(cols[:, None] - cols[None, :]).astype(np.float32).reshape(9 * CW, CW)
    high = row_ops.astype(BF16)
    low = (row_ops - high.astype(np.float32)).astype(BF16)
    return high, low, col_ops


def split(x):
    high = x.astype(BF16)
    return high, (x - high.astype(F32)).astype(BF16)


def dot(a, b):
    return jnp.dot(a, b, preferred_element_type=F32)


def kernel(
    flux_mode,
    mask_h, var_h, exp_h, coef_h, visit_h, patch_h, row_h, col_h, rhi_h, rlo_h, cop_h,
    *refs,
):
    if flux_mode:
        num_o, wgt_o, flag_o, *refs = refs
    else:
        wgt_o, *refs = refs
    (
        coef, visit_s, patch, row, col, col_s, mask, var, expo, rhi, rlo, cop,
        use, tmp, e_hi, e_lo, s_hi, s_lo, m_hi, m_lo, wk,
        hot, packed, msend, mrelay, arrived, mrecv, crep, vrep, rows_of, wide, rhs, placed,
        flag_out, flag_plane, flag_z, flag_band,
        load_sem, send_sem, data_sem, msem, flag_sem,
    ) = refs
    me = lax.axis_index("patch")
    band = lax.axis_index("band")
    my_plane = me // GROUP

    loads = {
        name: pltpu.make_async_copy(src, dst, load_sem.at[k])
        for k, (name, src, dst) in enumerate(
            [
                ("coefficients", coef_h, coef),
                ("column_taps", cop_h, cop),
                ("patch", patch_h, patch),
                ("mask", mask_h, mask),
                ("row", row_h, row),
                ("col", col_h, col),
                ("visit", visit_h, visit_s),
                ("col_scalar", col_h, col_s),
                ("variance", var_h, var),
                ("exposures", exp_h, expo),
                ("row_high", rhi_h, rhi),
                ("row_low", rlo_h, rlo),
            ]
        )
        if flux_mode or name not in FLUX_ONLY
    }
    for load in loads.values():
        load.start()

    barrier = pltpu.get_barrier_semaphore()

    def greet(k, c):
        pl.semaphore_signal(
            barrier, inc=1, device_id=(lax.rem(me + k, DEVS), band), device_id_type=MESH
        )
        return c

    lax.fori_loop(1, DEVS, greet, 0)
    if flux_mode:
        for k in range(1, BANDS):
            pl.semaphore_signal(
                barrier, inc=1, device_id=(me, lax.rem(band + k, BANDS)), device_id_type=MESH
            )
    greeted = DEVS - 1 + (BANDS - 1 if flux_mode else 0)

    if flux_mode:
        x = 2.0 * lax.broadcasted_iota(jnp.int32, (1, CW), 1).astype(F32) / (CW - 1) - 1.0
        loads["coefficients"].wait()
        basis = lax.broadcasted_iota(jnp.int32, (NB, NB), 0) == lax.broadcasted_iota(
            jnp.int32, (NB, NB), 1
        )

        def term(n, p):
            return jnp.sum(
                jnp.where(basis, jnp.broadcast_to(coef[p, n : n + 1, :], (NB, NB)), 0.0),
                axis=1,
                keepdims=True,
            )

        for n in range(CCDS):
            k = [term(n, p) for p in range(6)]
            wk[n, 0] = k[0] + k[1] * x + k[3] * (x * x)
            wk[n, 1] = k[2] + k[4] * x
            wk[n, 2] = jnp.broadcast_to(k[5], (NB, CW))
        loads["column_taps"].wait()

        def column_ops(k, c):
            to = pl.ds(k * CW, CW)
            for n in range(CCDS):
                for p in range(3):
                    m = jnp.zeros((CW, CW), F32)
                    for b in range(3):
                        at = pl.ds((k // 3 * 3 + b) * CW, CW)
                        m = m + cop[at, :] * wk[n, p, pl.ds(3 * k + b, 1), :]
                    high, low = split(m)
                    m_hi[n, to, p * CW : (p + 1) * CW] = high
                    m_lo[n, to, p * CW : (p + 1) * CW] = low
            return c

        for k in range(9):
            column_ops(k, 0)

    loads["patch"].wait()
    lane = lax.broadcasted_iota(jnp.int32, (STRIPS, STRIPS), 1)
    sub = lax.broadcasted_iota(jnp.int32, (STRIPS, STRIPS), 0)
    prow = patch[...]
    pfull = jnp.broadcast_to(prow, (STRIPS, STRIPS))
    pcol = jnp.sum(jnp.where(lane == sub, pfull, 0), axis=1, keepdims=True)
    rank = jnp.sum(
        jnp.where((pcol == pfull) & (sub < lane), 1, 0), axis=0, keepdims=True
    )
    slot = prow * SLOTS + rank
    slot_id = lax.broadcasted_iota(jnp.int32, (DEVS * SLOTS, STRIPS), 0)
    hot[...] = (slot_id == slot).astype(F32).astype(BF16)

    loads["mask"].wait()
    use[...] = jnp.where(jnp.bitwise_and(mask[...], 3) != 3, 1.0, 0.0)
    for name in ("row", "col", "col_scalar", "visit", "variance"):
        loads[name].wait()
    lane1 = lax.broadcasted_iota(jnp.int32, (1, CW), 1)
    sums = jnp.zeros((1, CW), F32)
    usable_count = 0.0
    for c in range(CCDS):
        u = use[c * CH : (c + 1) * CH, :]
        count = jnp.sum(u)
        amount = jnp.sum(u * var[c * CH : (c + 1) * CH, :])
        usable_count = usable_count + count
        v = visit_s[0, c]
        sums = sums + jnp.where(lane1 == v + 16, count, 0.0) + jnp.where(lane1 == v + 24, amount, 0.0)
    strip_lane = lax.broadcasted_iota(jnp.int32, (1, STRIPS), 1)
    vrow = jnp.where(strip_lane < STRIPS // CCDS, visit_s[0, 0], visit_s[0, 1])
    q_sub = lax.broadcasted_iota(jnp.int32, (CW, STRIPS), 0)
    hot_id = lax.broadcasted_iota(jnp.int32, (DEVS, STRIPS), 0)
    meta = jnp.broadcast_to(sums, (DEVS, CW))
    for j in range(SLOTS):
        q = jnp.where(q_sub == 8 * j, row[...], 0)
        q = jnp.where(q_sub == 8 * j + 1, col[...] - COL_SHIFT, q)
        q = jnp.where(q_sub == 8 * j + 2, vrow, q)
        hot_j = (hot_id * SLOTS + j == slot).astype(F32).astype(BF16)
        meta = meta + lax.dot_general(
            hot_j, q.astype(F32).astype(BF16), (((1,), (1,)), ((), ())), preferred_element_type=F32
        )
    msend[...] = meta.reshape(PLANES, GROUP, 1, CW)

    if flux_mode:
        loads["exposures"].wait()
        for c in range(CCDS):
            high, low = split(expo[c * CH : (c + 1) * CH, :])
            e_hi[:, c * CW : (c + 1) * CW] = high
            e_lo[:, c * CW : (c + 1) * CW] = low
        loads["row_high"].wait()
        loads["row_low"].wait()

        def row_pass(k, c):
            at = pl.ds(k * CH, CH)
            to = pl.ds(k * CW, CW)
            s = dot(rhi[at, :], e_hi[...]) + dot(rhi[at, :], e_lo[...]) + dot(rlo[at, :], e_hi[...])
            high, low = split(s)
            for n in range(CCDS):
                s_hi[n, :, to] = high[:, n * CW : (n + 1) * CW]
                s_lo[n, :, to] = low[:, n * CW : (n + 1) * CW]
            return c

        for k in range(9):
            row_pass(k, 0)

    pl.semaphore_wait(barrier, greeted)

    mine = lax.rem(me, GROUP)
    for k in range(1, PLANES):
        plane = lax.rem(my_plane + k, PLANES)
        pltpu.make_async_remote_copy(
            src_ref=msend.at[plane],
            dst_ref=mrelay.at[my_plane],
            send_sem=send_sem.at[1],
            recv_sem=msem.at[0],
            device_id=(plane * GROUP + mine, band),
            device_id_type=MESH,
        ).start()
    pltpu.make_async_copy(msend.at[my_plane], mrelay.at[my_plane], msem.at[0]).start()

    def relay_meta():
        pltpu.make_async_copy(msend, mrelay, msem.at[0]).wait()
        for k in range(1, GROUP):
            place = lax.rem(mine + k, GROUP)
            pltpu.make_async_remote_copy(
                src_ref=mrelay.at[:, place],
                dst_ref=mrecv.at[:, mine],
                send_sem=send_sem.at[2],
                recv_sem=msem.at[1],
                device_id=(my_plane * GROUP + place, band),
                device_id_type=MESH,
            ).start()
        pltpu.make_async_copy(mrelay.at[:, mine], mrecv.at[:, mine], msem.at[1]).start()

    if flux_mode:
        y = 2.0 * lax.broadcasted_iota(jnp.int32, (CH, 1), 0).astype(F32) / (CH - 1) - 1.0
        for n in range(CCDS):
            o = dot(s_hi[n], m_hi[n]) + dot(s_hi[n], m_lo[n]) + dot(s_lo[n], m_hi[n])
            conv = o[:, :CW] + y * o[:, CW : 2 * CW] + (y * y) * o[:, 2 * CW :]
            for k in range(CH // SR):
                at = pl.ds(n * CH + k * SR, SR)
                flux = use[at, :] * conv[k * SR : (k + 1) * SR, :]
                tmp[at, :] = pltpu.roll(
                    flux, lax.bitwise_and(col_s[0, n * (CH // SR) + k], CW - 1), 1
                )

    def roll_strip(s, c):
        at = pl.ds(pl.multiple_of(s * SR, SR), SR)
        tmp[at, :] = pltpu.roll(use[at, :], lax.bitwise_and(col_s[0, s], CW - 1), 1)
        return c

    if not flux_mode:
        lax.fori_loop(0, STRIPS, roll_strip, 0, unroll=8)
    for i in range(SR):
        high, low = split(tmp[pl.ds(i, STRIPS, stride=SR), :])
        packed[pl.ds(i, DEVS * SLOTS, stride=SR), :] = dot(hot[...], high) + dot(hot[...], low)

    def block(d):
        return pl.ds(pl.multiple_of(d * BLOCK, BLOCK), BLOCK)

    def send_half(half):
        def one(k, c):
            d = half * (DEVS // 2) + lax.rem(me + k, DEVS // 2)

            @pl.when(d != me)
            def _():
                pltpu.make_async_remote_copy(
                    src_ref=packed.at[block(d)],
                    dst_ref=arrived.at[block(me)],
                    send_sem=send_sem.at[0],
                    recv_sem=data_sem.at[my_plane],
                    device_id=(d, band),
                    device_id_type=MESH,
                ).start()

            return c

        lax.fori_loop(0, DEVS // 2, one, 0)

    send_half(0)
    relay_meta()
    send_half(1)
    pltpu.make_async_copy(
        packed.at[block(me)], arrived.at[block(me)], data_sem.at[my_plane]
    ).start()

    def flag_round(r, value, land, mine, peers):
        flag_out[r] = value
        land[mine] = value
        for device_id in peers:
            pltpu.make_async_remote_copy(
                src_ref=flag_out.at[r],
                dst_ref=land.at[mine],
                send_sem=flag_sem.at[0, r],
                recv_sem=flag_sem.at[1, r],
                device_id=device_id,
                device_id_type=MESH,
            ).start()

    def flag_end(r, land):
        n = land.shape[0] - 1
        for k in range(2):
            rest = land.at[pl.ds(0, n)]
            pltpu.make_async_copy(rest, rest, flag_sem.at[k, r]).wait()
        return jnp.max(land[...].reshape(n + 1, CW), axis=0, keepdims=True)

    if flux_mode:
        nonzero = jnp.sum(jnp.where(packed[...] != 0.0, 1.0, 0.0))
        flag = jnp.zeros((1, CW), F32) + (usable_count - nonzero)
        flag_round(
            0, flag, flag_plane, mine,
            [(my_plane * GROUP + lax.rem(mine + k, GROUP), band) for k in range(1, GROUP)],
        )

    pltpu.make_async_copy(mrelay, mrecv, msem.at[1]).wait()
    if flux_mode:
        flag_round(
            1, flag_end(0, flag_plane), flag_z, my_plane,
            [(lax.rem(me + k * GROUP, DEVS), band) for k in range(1, PLANES)],
        )
    got = mrecv[...].reshape(DEVS, CW)
    totals = jnp.sum(got, axis=0, keepdims=True)
    weights = (totals + 1.0) / (pltpu.roll(totals, CW - 8, 1) + 1.0)
    lane_d = lax.broadcasted_iota(jnp.int32, (DEVS, CW), 1)
    for j in range(SLOTS):
        at = pl.ds(j * DEVS, DEVS)
        v = got[:, 8 * j + 2 : 8 * j + 3].astype(jnp.int32)
        vw = jnp.sum(
            jnp.where(lane_d == v + 16, jnp.broadcast_to(weights, (DEVS, CW)), 0.0),
            axis=1,
            keepdims=True,
        )
        rhs[at, 0:CW] = jnp.broadcast_to(got[:, 8 * j + 1 : 8 * j + 2], (DEVS, CW))
        rhs[at, CW : 2 * CW] = jnp.broadcast_to(got[:, 8 * j : 8 * j + 1], (DEVS, CW))
        rhs[at, 2 * CW :] = jnp.broadcast_to(vw, (DEVS, CW))
    spread_in = rhs[...].astype(BF16)
    weights_low = split(rhs[:, 2 * CW :])[1]

    k_sub = lax.broadcasted_iota(jnp.int32, (CHUNK, SLOTS * DEVS), 0)
    k_lane = lax.broadcasted_iota(jnp.int32, (CHUNK, SLOTS * DEVS), 1)
    lane_c = lax.broadcasted_iota(jnp.int32, (CHUNK, CW), 1).astype(F32)
    row_in = (lax.broadcasted_iota(jnp.int32, (CHUNK, CW), 0) % SR).astype(F32)

    def spread(p, c):
        at = pl.ds(pl.multiple_of(p * CHUNK, CHUNK), CHUNK)
        here = (k_lane - p * GROUP == k_sub // BLOCK + (k_sub // SR) % SLOTS * DEVS)
        here = here.astype(F32).astype(BF16)
        full = dot(here, spread_in)
        crep[at, :] = lane_c - (full[:, :CW] + COL_SHIFT)
        rt = (lane_c == full[:, CW : 2 * CW] + row_in).astype(F32)
        turned = jnp.transpose(rt).astype(BF16)
        rows_of[p, :, 0:CHUNK] = turned
        rows_of[p, :, CHUNK : 2 * CHUNK] = turned
        vrep[at, :] = full[:, 2 * CW :] + dot(here, weights_low)
        return c

    lax.fori_loop(0, PLANES, spread, 0)
    if flux_mode:
        flag_round(
            2, flag_end(1, flag_z), flag_band, band,
            [(me, lax.rem(band + k, BANDS)) for k in range(1, BANDS)],
        )

    placed[...] = jnp.zeros_like(placed)

    def place(p, c):
        at = pl.ds(pl.multiple_of(p * CHUNK, CHUNK), CHUNK)
        pltpu.make_async_copy(packed.at[at], arrived.at[at], data_sem.at[p]).wait()
        value = arrived[at, :]
        weight = vrep[at, :]
        maps = [value * weight]
        if flux_mode:
            maps.append(jnp.where(value != 0.0, weight, 0.0))
        off = crep[at, :]
        for n, (high, low) in enumerate(split(m) for m in maps):
            zero = jnp.zeros_like(high)
            for t in range(PW // CW):
                away = off + float(t * CW)
                inside = (away >= 0.0) & (away < CW)
                cols = pl.ds(n * PW + t * CW, CW)
                wide[0:CHUNK, cols] = jnp.where(inside, high, zero)
                wide[CHUNK : 2 * CHUNK, cols] = jnp.where(inside, low, zero)
        placed[...] += dot(rows_of[p], wide[...])
        return c

    lax.fori_loop(0, PLANES, place, 0)
    if flux_mode:
        num_o[...] = placed[:, :PW]
        wgt_o[...] = placed[:, PW:]
        flag_o[...] = flag_end(2, flag_band)
    else:
        wgt_o[...] = placed[...]

    for k in (1, 2):
        others = mrelay.at[pl.ds(0, PLANES - 1)]
        pltpu.make_async_copy(others, others, send_sem.at[k]).wait()
    rest = packed.at[pl.ds(0, (DEVS - 1) * BLOCK)]
    pltpu.make_async_copy(rest, rest, send_sem.at[0]).wait()


def exchange(flux_mode, operands):
    slots = DEVS * BLOCK
    flat = (CCDS * CH, CW)
    hbm = pl.BlockSpec(memory_space=pltpu.HBM)
    vmem = pl.BlockSpec(memory_space=pltpu.VMEM)
    image = jax.ShapeDtypeStruct((PH, PW), F32)
    outs = [image, image, jax.ShapeDtypeStruct((1, CW), F32)] if flux_mode else [image]
    maps = 2 if flux_mode else 1
    return pl.pallas_call(
        functools.partial(kernel, flux_mode),
        out_shape=outs,
        in_specs=[hbm] * 11,
        out_specs=[vmem] * len(outs),
        scratch_shapes=[
            pltpu.VMEM((6, CCDS, NB), F32),
            pltpu.SMEM((1, CCDS), jnp.int32),
            pltpu.VMEM((1, STRIPS), jnp.int32),
            pltpu.VMEM((1, STRIPS), jnp.int32),
            pltpu.VMEM((1, STRIPS), jnp.int32),
            pltpu.SMEM((1, STRIPS), jnp.int32),
            pltpu.VMEM(flat, jnp.int32),
            pltpu.VMEM(flat, F32),
            pltpu.VMEM(flat, F32),
            pltpu.VMEM((9 * CH, CH), BF16),
            pltpu.VMEM((9 * CH, CH), BF16),
            pltpu.VMEM((9 * CW, CW), F32),
            pltpu.VMEM(flat, F32),
            pltpu.VMEM(flat, F32),
            pltpu.VMEM((CH, CCDS * CW), BF16),
            pltpu.VMEM((CH, CCDS * CW), BF16),
            pltpu.VMEM((CCDS, CH, 9 * CW), BF16),
            pltpu.VMEM((CCDS, CH, 9 * CW), BF16),
            pltpu.VMEM((CCDS, 9 * CW, 3 * CW), BF16),
            pltpu.VMEM((CCDS, 9 * CW, 3 * CW), BF16),
            pltpu.VMEM((CCDS, 3, NB, CW), F32),
            pltpu.VMEM((DEVS * SLOTS, STRIPS), BF16),
            pltpu.VMEM((slots, CW), F32),
            pltpu.VMEM((PLANES, GROUP, 1, CW), F32),
            pltpu.VMEM((PLANES, GROUP, 1, CW), F32),
            pltpu.VMEM((slots, CW), F32),
            pltpu.VMEM((PLANES, GROUP, 1, CW), F32),
            pltpu.VMEM((slots, CW), F32),
            pltpu.VMEM((slots, CW), F32),
            pltpu.VMEM((PLANES, PH, 2 * CHUNK), BF16),
            pltpu.VMEM((2 * CHUNK, maps * PW), BF16),
            pltpu.VMEM((SLOTS * DEVS, 3 * CW), F32),
            pltpu.VMEM((PH, maps * PW), F32),
            pltpu.VMEM((3, 1, CW), F32),
            pltpu.VMEM((GROUP, 1, CW), F32),
            pltpu.VMEM((PLANES, 1, CW), F32),
            pltpu.VMEM((BANDS, 1, CW), F32),
            pltpu.SemaphoreType.DMA((12,)),
            pltpu.SemaphoreType.DMA((3,)),
            pltpu.SemaphoreType.DMA((PLANES,)),
            pltpu.SemaphoreType.DMA((2,)),
            pltpu.SemaphoreType.DMA((2, 3)),
        ],
        compiler_params=pltpu.CompilerParams(
            collective_id=0 if flux_mode else 1,
            has_side_effects=True,
            vmem_limit_bytes=40 * 1024 * 1024,
        ),
        cost_estimate=pl.CostEstimate(
            flops=2_600_000_000, bytes_accessed=6_000_000, transcendentals=0
        ),
    )(*(pltpu.with_memory_space_constraint(operand, pltpu.HBM) for operand in operands))


def shards(
    exposures, variance, mask_bits, kernel_coeffs, ccd_visit, strip_patch, strip_row, strip_col
):
    rhi, rlo, cop = tap_matrices()
    flat = (CCDS * CH, CW)
    operands = (
        mask_bits.reshape(flat),
        variance.reshape(flat),
        exposures.reshape(flat),
        kernel_coeffs.transpose(2, 0, 1),
        ccd_visit.reshape(1, CCDS),
        strip_patch.reshape(1, STRIPS),
        strip_row.reshape(1, STRIPS),
        strip_col.reshape(1, STRIPS),
        jnp.asarray(rhi),
        jnp.asarray(rlo),
        jnp.asarray(cop),
    )
    num, wgt, flag = exchange(True, operands)

    def finish(num, wgt):
        return (num / jnp.maximum(wgt, 1.0))[None], jnp.maximum(wgt, 0.0)[None]

    return lax.cond(
        flag[0, 0] > 0.0,
        lambda: finish(num, exchange(False, operands)[0]),
        lambda: finish(num, wgt),
    )


def solution(mesh):
    return jax.shard_map(
        shards,
        mesh=mesh,
        in_specs=(
            P(("band", "patch"), None, None),
            P(("band", "patch"), None, None),
            P(("band", "patch"), None, None),
            P(("band", "patch"), None, None),
            P(("band", "patch"), None),
            P(("band", "patch"), None),
            P(("band", "patch")),
            P(("band", "patch")),
        ),
        out_specs=(P(("band", "patch"), None, None), P(("band", "patch"), None, None)),
        check_vma=False,
    )
```

```python
import functools

import jax
import jax.numpy as jnp
import numpy as np
from jax import lax
from jax.experimental import pallas as pl
from jax.experimental.pallas import tpu as pltpu
from jax.sharding import PartitionSpec as P

PH = 128
PW = 512
KS = 21
VISITS = 8
GAUSS_WIDTHS = (0.75, 1.5, 3.0)
MESH = pl.DeviceIdType.MESH
F32 = jnp.float32
BF16 = jnp.bfloat16

CCDS = 2
CH = 256
CW = 128
SR = 8
STRIPS = 64
DEVS = 64
NB = 27
SLOTS = 2
BLOCK = SLOTS * SR
PLANES = 8
GROUP = DEVS // PLANES
BANDS = 4
FLUX_ONLY = ("exposures", "row_high", "row_low", "coefficients", "column_taps")
CHUNK = GROUP * BLOCK
COL_SHIFT = 192


def taps(offsets):
    half = KS // 2
    support = np.arange(-half, half + 1, dtype=np.float64)
    inside = np.abs(offsets) <= half
    tables = []
    for spread in GAUSS_WIDTHS:
        total = np.sum(np.exp(-support * support / (2.0 * spread * spread)))
        profile = np.where(inside, np.exp(-offsets * offsets / (2.0 * spread * spread)) / total, 0.0)
        scaled = offsets / spread
        tables += [profile, profile * scaled, profile * scaled * scaled]
    return np.stack(tables)


def tap_matrices():
    rows = np.arange(CH, dtype=np.float64)
    row_ops = taps(rows[None, :] - rows[:, None]).astype(np.float32).reshape(9 * CH, CH)
    cols = np.arange(CW, dtype=np.float64)
    col_ops = taps(cols[:, None] - cols[None, :]).astype(np.float32).reshape(9 * CW, CW)
    high = row_ops.astype(BF16)
    low = (row_ops - high.astype(np.float32)).astype(BF16)
    return high, low, col_ops


def split(x):
    high = x.astype(BF16)
    return high, (x - high.astype(F32)).astype(BF16)


def halves(x):
    scaled = x * 4097.0
    high = scaled - (scaled - x)
    return high, x - high


def product(a, b):
    p = a * b
    a_high, a_low = halves(a)
    b_high, b_low = halves(b)
    return p, ((a_high * b_high - p) + a_high * b_low + a_low * b_high) + a_low * b_low


def dot(a, b):
    return jnp.dot(a, b, preferred_element_type=F32)


def kernel(
    flux_mode,
    mask_h, var_h, exp_h, coef_h, visit_h, patch_h, row_h, col_h, rhi_h, rlo_h, cop_h,
    *refs,
):
    if flux_mode:
        num_o, wgt_o, flag_o, *refs = refs
    else:
        wgt_o, *refs = refs
    (
        coef, visit_s, patch, row, col, col_s, mask, var, expo, rhi, rlo, cop,
        use, tmp, e_hi, e_lo, s_hi, s_lo, m_hi, m_lo, wk,
        hot, packed, msend, mrelay, arrived, mrecv, crep, vrep, rows_of, wide, rhs, placed,
        flag_out, flag_plane, flag_z, flag_band,
        load_sem, send_sem, data_sem, msem, flag_sem,
    ) = refs
    me = lax.axis_index("patch")
    band = lax.axis_index("band")
    my_plane = me // GROUP

    loads = {
        name: pltpu.make_async_copy(src, dst, load_sem.at[k])
        for k, (name, src, dst) in enumerate(
            [
                ("coefficients", coef_h, coef),
                ("column_taps", cop_h, cop),
                ("patch", patch_h, patch),
                ("mask", mask_h, mask),
                ("row", row_h, row),
                ("col", col_h, col),
                ("visit", visit_h, visit_s),
                ("col_scalar", col_h, col_s),
                ("variance", var_h, var),
                ("exposures", exp_h, expo),
                ("row_high", rhi_h, rhi),
                ("row_low", rlo_h, rlo),
            ]
        )
        if flux_mode or name not in FLUX_ONLY
    }
    for load in loads.values():
        load.start()

    barrier = pltpu.get_barrier_semaphore()

    def greet(k, c):
        pl.semaphore_signal(
            barrier, inc=1, device_id=(lax.rem(me + k, DEVS), band), device_id_type=MESH
        )
        return c

    lax.fori_loop(1, DEVS, greet, 0)
    if flux_mode:
        for k in range(1, BANDS):
            pl.semaphore_signal(
                barrier, inc=1, device_id=(me, lax.rem(band + k, BANDS)), device_id_type=MESH
            )
    greeted = DEVS - 1 + (BANDS - 1 if flux_mode else 0)

    if flux_mode:
        x = 2.0 * lax.broadcasted_iota(jnp.int32, (1, CW), 1).astype(F32) / (CW - 1) - 1.0
        loads["coefficients"].wait()
        basis = lax.broadcasted_iota(jnp.int32, (NB, NB), 0) == lax.broadcasted_iota(
            jnp.int32, (NB, NB), 1
        )

        def term(n, p):
            return jnp.sum(
                jnp.where(basis, jnp.broadcast_to(coef[p, n : n + 1, :], (NB, NB)), 0.0),
                axis=1,
                keepdims=True,
            )

        for n in range(CCDS):
            k = [term(n, p) for p in range(6)]
            wk[n, 0] = k[0] + k[1] * x + k[3] * (x * x)
            wk[n, 1] = k[2] + k[4] * x
            wk[n, 2] = jnp.broadcast_to(k[5], (NB, CW))
        loads["column_taps"].wait()

        def column_ops(k, c):
            to = pl.ds(k * CW, CW)
            for n in range(CCDS):
                for p in range(3):
                    m = jnp.zeros((CW, CW), F32)
                    for b in range(3):
                        at = pl.ds((k // 3 * 3 + b) * CW, CW)
                        m = m + cop[at, :] * wk[n, p, pl.ds(3 * k + b, 1), :]
                    high, low = split(m)
                    m_hi[n, to, p * CW : (p + 1) * CW] = high
                    m_lo[n, to, p * CW : (p + 1) * CW] = low
            return c

        for k in range(9):
            column_ops(k, 0)

    loads["patch"].wait()
    lane = lax.broadcasted_iota(jnp.int32, (STRIPS, STRIPS), 1)
    sub = lax.broadcasted_iota(jnp.int32, (STRIPS, STRIPS), 0)
    prow = patch[...]
    pfull = jnp.broadcast_to(prow, (STRIPS, STRIPS))
    pcol = jnp.sum(jnp.where(lane == sub, pfull, 0), axis=1, keepdims=True)
    rank = jnp.sum(
        jnp.where((pcol == pfull) & (sub < lane), 1, 0), axis=0, keepdims=True
    )
    slot = prow * SLOTS + rank
    slot_id = lax.broadcasted_iota(jnp.int32, (DEVS * SLOTS, STRIPS), 0)
    hot[...] = (slot_id == slot).astype(F32).astype(BF16)

    loads["mask"].wait()
    use[...] = jnp.where(jnp.bitwise_and(mask[...], 3) != 3, 1.0, 0.0)
    for name in ("row", "col", "col_scalar", "visit", "variance"):
        loads[name].wait()
    lane1 = lax.broadcasted_iota(jnp.int32, (1, CW), 1)
    sums = jnp.zeros((1, CW), F32)
    usable_count = 0.0
    for c in range(CCDS):
        u = use[c * CH : (c + 1) * CH, :]
        count = jnp.sum(u)
        amount = jnp.sum(u * var[c * CH : (c + 1) * CH, :])
        usable_count = usable_count + count
        v = visit_s[0, c]
        sums = sums + jnp.where(lane1 == v + 16, count, 0.0) + jnp.where(lane1 == v + 24, amount, 0.0)
    strip_lane = lax.broadcasted_iota(jnp.int32, (1, STRIPS), 1)
    vrow = jnp.where(strip_lane < STRIPS // CCDS, visit_s[0, 0], visit_s[0, 1])
    q_sub = lax.broadcasted_iota(jnp.int32, (CW, STRIPS), 0)
    hot_id = lax.broadcasted_iota(jnp.int32, (DEVS, STRIPS), 0)
    meta = jnp.broadcast_to(sums, (DEVS, CW))
    for j in range(SLOTS):
        q = jnp.where(q_sub == 8 * j, row[...], 0)
        q = jnp.where(q_sub == 8 * j + 1, col[...] - COL_SHIFT, q)
        q = jnp.where(q_sub == 8 * j + 2, vrow, q)
        hot_j = (hot_id * SLOTS + j == slot).astype(F32).astype(BF16)
        meta = meta + lax.dot_general(
            hot_j, q.astype(F32).astype(BF16), (((1,), (1,)), ((), ())), preferred_element_type=F32
        )
    msend[...] = meta.reshape(PLANES, GROUP, 1, CW)

    if flux_mode:
        loads["exposures"].wait()
        for c in range(CCDS):
            high, low = split(expo[c * CH : (c + 1) * CH, :])
            e_hi[:, c * CW : (c + 1) * CW] = high
            e_lo[:, c * CW : (c + 1) * CW] = low
        loads["row_high"].wait()
        loads["row_low"].wait()

        def row_pass(k, c):
            at = pl.ds(k * CH, CH)
            to = pl.ds(k * CW, CW)
            s = dot(rhi[at, :], e_hi[...]) + dot(rhi[at, :], e_lo[...]) + dot(rlo[at, :], e_hi[...])
            high, low = split(s)
            for n in range(CCDS):
                s_hi[n, :, to] = high[:, n * CW : (n + 1) * CW]
                s_lo[n, :, to] = low[:, n * CW : (n + 1) * CW]
            return c

        for k in range(9):
            row_pass(k, 0)

    pl.semaphore_wait(barrier, greeted)

    mine = lax.rem(me, GROUP)
    for k in range(1, PLANES):
        plane = lax.rem(my_plane + k, PLANES)
        pltpu.make_async_remote_copy(
            src_ref=msend.at[plane],
            dst_ref=mrelay.at[my_plane],
            send_sem=send_sem.at[1],
            recv_sem=msem.at[0],
            device_id=(plane * GROUP + mine, band),
            device_id_type=MESH,
        ).start()
    pltpu.make_async_copy(msend.at[my_plane], mrelay.at[my_plane], msem.at[0]).start()

    def relay_meta():
        pltpu.make_async_copy(msend, mrelay, msem.at[0]).wait()
        for k in range(1, GROUP):
            place = lax.rem(mine + k, GROUP)
            pltpu.make_async_remote_copy(
                src_ref=mrelay.at[:, place],
                dst_ref=mrecv.at[:, mine],
                send_sem=send_sem.at[2],
                recv_sem=msem.at[1],
                device_id=(my_plane * GROUP + place, band),
                device_id_type=MESH,
            ).start()
        pltpu.make_async_copy(mrelay.at[:, mine], mrecv.at[:, mine], msem.at[1]).start()

    if flux_mode:
        y = 2.0 * lax.broadcasted_iota(jnp.int32, (CH, 1), 0).astype(F32) / (CH - 1) - 1.0
        for n in range(CCDS):
            o = dot(s_hi[n], m_hi[n]) + dot(s_hi[n], m_lo[n]) + dot(s_lo[n], m_hi[n])
            first, first_rest = product(y, o[:, CW : 2 * CW])
            second, second_rest = product(y * y, o[:, 2 * CW :])
            conv = (o[:, :CW] + first + second) + (first_rest + second_rest)
            for k in range(CH // SR):
                at = pl.ds(n * CH + k * SR, SR)
                flux = use[at, :] * conv[k * SR : (k + 1) * SR, :]
                tmp[at, :] = pltpu.roll(
                    flux, lax.bitwise_and(col_s[0, n * (CH // SR) + k], CW - 1), 1
                )

    def roll_strip(s, c):
        at = pl.ds(pl.multiple_of(s * SR, SR), SR)
        tmp[at, :] = pltpu.roll(use[at, :], lax.bitwise_and(col_s[0, s], CW - 1), 1)
        return c

    if not flux_mode:
        lax.fori_loop(0, STRIPS, roll_strip, 0, unroll=8)
    for i in range(SR):
        high, low = split(tmp[pl.ds(i, STRIPS, stride=SR), :])
        packed[pl.ds(i, DEVS * SLOTS, stride=SR), :] = dot(hot[...], high) + dot(hot[...], low)

    def block(d):
        return pl.ds(pl.multiple_of(d * BLOCK, BLOCK), BLOCK)

    def send_half(half):
        def one(k, c):
            d = half * (DEVS // 2) + lax.rem(me + k, DEVS // 2)

            @pl.when(d != me)
            def _():
                pltpu.make_async_remote_copy(
                    src_ref=packed.at[block(d)],
                    dst_ref=arrived.at[block(me)],
                    send_sem=send_sem.at[0],
                    recv_sem=data_sem.at[my_plane],
                    device_id=(d, band),
                    device_id_type=MESH,
                ).start()

            return c

        lax.fori_loop(0, DEVS // 2, one, 0)

    send_half(0)
    relay_meta()
    send_half(1)
    pltpu.make_async_copy(
        packed.at[block(me)], arrived.at[block(me)], data_sem.at[my_plane]
    ).start()

    def flag_round(r, value, land, mine, peers):
        flag_out[r] = value
        land[mine] = value
        for device_id in peers:
            pltpu.make_async_remote_copy(
                src_ref=flag_out.at[r],
                dst_ref=land.at[mine],
                send_sem=flag_sem.at[0, r],
                recv_sem=flag_sem.at[1, r],
                device_id=device_id,
                device_id_type=MESH,
            ).start()

    def flag_end(r, land):
        n = land.shape[0] - 1
        for k in range(2):
            rest = land.at[pl.ds(0, n)]
            pltpu.make_async_copy(rest, rest, flag_sem.at[k, r]).wait()
        return jnp.max(land[...].reshape(n + 1, CW), axis=0, keepdims=True)

    if flux_mode:
        nonzero = jnp.sum(jnp.where(packed[...] != 0.0, 1.0, 0.0))
        flag = jnp.zeros((1, CW), F32) + (usable_count - nonzero)
        flag_round(
            0, flag, flag_plane, mine,
            [(my_plane * GROUP + lax.rem(mine + k, GROUP), band) for k in range(1, GROUP)],
        )

    pltpu.make_async_copy(mrelay, mrecv, msem.at[1]).wait()
    if flux_mode:
        flag_round(
            1, flag_end(0, flag_plane), flag_z, my_plane,
            [(lax.rem(me + k * GROUP, DEVS), band) for k in range(1, PLANES)],
        )
    got = mrecv[...].reshape(DEVS, CW)
    totals = jnp.sum(got, axis=0, keepdims=True)
    weights = (totals + 1.0) / (pltpu.roll(totals, CW - 8, 1) + 1.0)
    lane_d = lax.broadcasted_iota(jnp.int32, (DEVS, CW), 1)
    for j in range(SLOTS):
        at = pl.ds(j * DEVS, DEVS)
        v = got[:, 8 * j + 2 : 8 * j + 3].astype(jnp.int32)
        vw = jnp.sum(
            jnp.where(lane_d == v + 16, jnp.broadcast_to(weights, (DEVS, CW)), 0.0),
            axis=1,
            keepdims=True,
        )
        rhs[at, 0:CW] = jnp.broadcast_to(got[:, 8 * j + 1 : 8 * j + 2], (DEVS, CW))
        rhs[at, CW : 2 * CW] = jnp.broadcast_to(got[:, 8 * j : 8 * j + 1], (DEVS, CW))
        rhs[at, 2 * CW :] = jnp.broadcast_to(vw, (DEVS, CW))
    spread_in = rhs[...].astype(BF16)
    weights_low = split(rhs[:, 2 * CW :])[1]

    k_sub = lax.broadcasted_iota(jnp.int32, (CHUNK, SLOTS * DEVS), 0)
    k_lane = lax.broadcasted_iota(jnp.int32, (CHUNK, SLOTS * DEVS), 1)
    lane_c = lax.broadcasted_iota(jnp.int32, (CHUNK, CW), 1).astype(F32)
    row_in = (lax.broadcasted_iota(jnp.int32, (CHUNK, CW), 0) % SR).astype(F32)

    def spread(p, c):
        at = pl.ds(pl.multiple_of(p * CHUNK, CHUNK), CHUNK)
        here = (k_lane - p * GROUP == k_sub // BLOCK + (k_sub // SR) % SLOTS * DEVS)
        here = here.astype(F32).astype(BF16)
        full = dot(here, spread_in)
        crep[at, :] = lane_c - (full[:, :CW] + COL_SHIFT)
        rt = (lane_c == full[:, CW : 2 * CW] + row_in).astype(F32)
        turned = jnp.transpose(rt).astype(BF16)
        rows_of[p, :, 0:CHUNK] = turned
        rows_of[p, :, CHUNK : 2 * CHUNK] = turned
        vrep[at, :] = full[:, 2 * CW :] + dot(here, weights_low)
        return c

    lax.fori_loop(0, PLANES, spread, 0)
    if flux_mode:
        flag_round(
            2, flag_end(1, flag_z), flag_band, band,
            [(me, lax.rem(band + k, BANDS)) for k in range(1, BANDS)],
        )

    placed[...] = jnp.zeros_like(placed)

    def place(p, c):
        at = pl.ds(pl.multiple_of(p * CHUNK, CHUNK), CHUNK)
        pltpu.make_async_copy(packed.at[at], arrived.at[at], data_sem.at[p]).wait()
        value = arrived[at, :]
        weight = vrep[at, :]
        maps = [value * weight]
        if flux_mode:
            maps.append(jnp.where(value != 0.0, weight, 0.0))
        off = crep[at, :]
        for n, (high, low) in enumerate(split(m) for m in maps):
            zero = jnp.zeros_like(high)
            for t in range(PW // CW):
                away = off + float(t * CW)
                inside = (away >= 0.0) & (away < CW)
                cols = pl.ds(n * PW + t * CW, CW)
                wide[0:CHUNK, cols] = jnp.where(inside, high, zero)
                wide[CHUNK : 2 * CHUNK, cols] = jnp.where(inside, low, zero)
        placed[...] += dot(rows_of[p], wide[...])
        return c

    lax.fori_loop(0, PLANES, place, 0)
    if flux_mode:
        num_o[...] = placed[:, :PW]
        wgt_o[...] = placed[:, PW:]
        flag_o[...] = flag_end(2, flag_band)
    else:
        wgt_o[...] = placed[...]

    for k in (1, 2):
        others = mrelay.at[pl.ds(0, PLANES - 1)]
        pltpu.make_async_copy(others, others, send_sem.at[k]).wait()
    rest = packed.at[pl.ds(0, (DEVS - 1) * BLOCK)]
    pltpu.make_async_copy(rest, rest, send_sem.at[0]).wait()


def exchange(flux_mode, operands):
    slots = DEVS * BLOCK
    flat = (CCDS * CH, CW)
    hbm = pl.BlockSpec(memory_space=pltpu.HBM)
    vmem = pl.BlockSpec(memory_space=pltpu.VMEM)
    image = jax.ShapeDtypeStruct((PH, PW), F32)
    outs = [image, image, jax.ShapeDtypeStruct((1, CW), F32)] if flux_mode else [image]
    maps = 2 if flux_mode else 1
    return pl.pallas_call(
        functools.partial(kernel, flux_mode),
        out_shape=outs,
        in_specs=[hbm] * 11,
        out_specs=[vmem] * len(outs),
        scratch_shapes=[
            pltpu.VMEM((6, CCDS, NB), F32),
            pltpu.SMEM((1, CCDS), jnp.int32),
            pltpu.VMEM((1, STRIPS), jnp.int32),
            pltpu.VMEM((1, STRIPS), jnp.int32),
            pltpu.VMEM((1, STRIPS), jnp.int32),
            pltpu.SMEM((1, STRIPS), jnp.int32),
            pltpu.VMEM(flat, jnp.int32),
            pltpu.VMEM(flat, F32),
            pltpu.VMEM(flat, F32),
            pltpu.VMEM((9 * CH, CH), BF16),
            pltpu.VMEM((9 * CH, CH), BF16),
            pltpu.VMEM((9 * CW, CW), F32),
            pltpu.VMEM(flat, F32),
            pltpu.VMEM(flat, F32),
            pltpu.VMEM((CH, CCDS * CW), BF16),
            pltpu.VMEM((CH, CCDS * CW), BF16),
            pltpu.VMEM((CCDS, CH, 9 * CW), BF16),
            pltpu.VMEM((CCDS, CH, 9 * CW), BF16),
            pltpu.VMEM((CCDS, 9 * CW, 3 * CW), BF16),
            pltpu.VMEM((CCDS, 9 * CW, 3 * CW), BF16),
            pltpu.VMEM((CCDS, 3, NB, CW), F32),
            pltpu.VMEM((DEVS * SLOTS, STRIPS), BF16),
            pltpu.VMEM((slots, CW), F32),
            pltpu.VMEM((PLANES, GROUP, 1, CW), F32),
            pltpu.VMEM((PLANES, GROUP, 1, CW), F32),
            pltpu.VMEM((slots, CW), F32),
            pltpu.VMEM((PLANES, GROUP, 1, CW), F32),
            pltpu.VMEM((slots, CW), F32),
            pltpu.VMEM((slots, CW), F32),
            pltpu.VMEM((PLANES, PH, 2 * CHUNK), BF16),
            pltpu.VMEM((2 * CHUNK, maps * PW), BF16),
            pltpu.VMEM((SLOTS * DEVS, 3 * CW), F32),
            pltpu.VMEM((PH, maps * PW), F32),
            pltpu.VMEM((3, 1, CW), F32),
            pltpu.VMEM((GROUP, 1, CW), F32),
            pltpu.VMEM((PLANES, 1, CW), F32),
            pltpu.VMEM((BANDS, 1, CW), F32),
            pltpu.SemaphoreType.DMA((12,)),
            pltpu.SemaphoreType.DMA((3,)),
            pltpu.SemaphoreType.DMA((PLANES,)),
            pltpu.SemaphoreType.DMA((2,)),
            pltpu.SemaphoreType.DMA((2, 3)),
        ],
        compiler_params=pltpu.CompilerParams(
            collective_id=0 if flux_mode else 1,
            has_side_effects=True,
            vmem_limit_bytes=40 * 1024 * 1024,
        ),
        cost_estimate=pl.CostEstimate(
            flops=2_600_000_000, bytes_accessed=6_000_000, transcendentals=0
        ),
    )(*(pltpu.with_memory_space_constraint(operand, pltpu.HBM) for operand in operands))


def shards(
    exposures, variance, mask_bits, kernel_coeffs, ccd_visit, strip_patch, strip_row, strip_col
):
    rhi, rlo, cop = tap_matrices()
    flat = (CCDS * CH, CW)
    operands = (
        mask_bits.reshape(flat),
        variance.reshape(flat),
        exposures.reshape(flat),
        kernel_coeffs.transpose(2, 0, 1),
        ccd_visit.reshape(1, CCDS),
        strip_patch.reshape(1, STRIPS),
        strip_row.reshape(1, STRIPS),
        strip_col.reshape(1, STRIPS),
        jnp.asarray(rhi),
        jnp.asarray(rlo),
        jnp.asarray(cop),
    )
    num, wgt, flag = exchange(True, operands)

    def finish(num, wgt):
        return (num / jnp.maximum(wgt, 1.0))[None], jnp.maximum(wgt, 0.0)[None]

    return lax.cond(
        flag[0, 0] > 0.0,
        lambda: finish(num, exchange(False, operands)[0]),
        lambda: finish(num, wgt),
    )


def solution(mesh):
    return jax.shard_map(
        shards,
        mesh=mesh,
        in_specs=(
            P(("band", "patch"), None, None),
            P(("band", "patch"), None, None),
            P(("band", "patch"), None, None),
            P(("band", "patch"), None, None),
            P(("band", "patch"), None),
            P(("band", "patch"), None),
            P(("band", "patch")),
            P(("band", "patch")),
        ),
        out_specs=(P(("band", "patch"), None, None), P(("band", "patch"), None, None)),
        check_vma=False,
    )
```

```python
import functools

import jax
import jax.numpy as jnp
import numpy as np
from jax import lax
from jax.experimental import pallas as pl
from jax.experimental.pallas import tpu as pltpu
from jax.sharding import PartitionSpec as P

PH = 128
PW = 512
KS = 21
VISITS = 8
GAUSS_WIDTHS = (0.75, 1.5, 3.0)
MESH = pl.DeviceIdType.MESH
F32 = jnp.float32
BF16 = jnp.bfloat16

CCDS = 2
CH = 256
CW = 128
SR = 8
STRIPS = 64
DEVS = 64
NB = 27
SLOTS = 2
BLOCK = SLOTS * SR
PLANES = 8
GROUP = DEVS // PLANES
BANDS = 4
FLUX_ONLY = ("exposures", "row_high", "row_low", "coefficients", "column_taps")
CHUNK = GROUP * BLOCK
COL_SHIFT = 192


def taps(offsets):
    half = KS // 2
    support = np.arange(-half, half + 1, dtype=np.float64)
    inside = np.abs(offsets) <= half
    tables = []
    for spread in GAUSS_WIDTHS:
        total = np.sum(np.exp(-support * support / (2.0 * spread * spread)))
        profile = np.where(inside, np.exp(-offsets * offsets / (2.0 * spread * spread)) / total, 0.0)
        scaled = offsets / spread
        tables += [profile, profile * scaled, profile * scaled * scaled]
    return np.stack(tables)


def tap_matrices():
    rows = np.arange(CH, dtype=np.float64)
    row_ops = taps(rows[None, :] - rows[:, None]).astype(np.float32).reshape(9 * CH, CH)
    cols = np.arange(CW, dtype=np.float64)
    col_ops = taps(cols[:, None] - cols[None, :]).astype(np.float32).reshape(9 * CW, CW)
    high = row_ops.astype(BF16)
    low = (row_ops - high.astype(np.float32)).astype(BF16)
    return high, low, col_ops


def split(x):
    high = x.astype(BF16)
    return high, (x - high.astype(F32)).astype(BF16)


def halves(x):
    scaled = x * 4097.0
    high = scaled - (scaled - x)
    return high, x - high


def product(a, b):
    p = a * b
    a_high, a_low = halves(a)
    b_high, b_low = halves(b)
    return p, ((a_high * b_high - p) + a_high * b_low + a_low * b_high) + a_low * b_low


def dot(a, b):
    return jnp.dot(a, b, preferred_element_type=F32)


def kernel(
    flux_mode,
    mask_h, var_h, exp_h, coef_h, visit_h, patch_h, row_h, col_h, rhi_h, rlo_h, cop_h,
    *refs,
):
    if flux_mode:
        num_o, wgt_o, flag_o, *refs = refs
    else:
        wgt_o, *refs = refs
    (
        coef, visit_s, patch, row, col, col_s, mask, var, expo, rhi, rlo, cop,
        use, tmp, e_hi, e_lo, s_hi, s_lo, m_hi, m_lo, wk,
        hot, packed, msend, mrelay, arrived, mrecv, crep, vrep, rows_of, wide, rhs, placed,
        flag_out, flag_plane, flag_z, flag_band,
        load_sem, send_sem, data_sem, msem, flag_sem,
    ) = refs
    me = lax.axis_index("patch")
    band = lax.axis_index("band")
    my_plane = me // GROUP

    loads = {
        name: pltpu.make_async_copy(src, dst, load_sem.at[k])
        for k, (name, src, dst) in enumerate(
            [
                ("coefficients", coef_h, coef),
                ("column_taps", cop_h, cop),
                ("patch", patch_h, patch),
                ("mask", mask_h, mask),
                ("row", row_h, row),
                ("col", col_h, col),
                ("visit", visit_h, visit_s),
                ("col_scalar", col_h, col_s),
                ("variance", var_h, var),
                ("exposures", exp_h, expo),
                ("row_high", rhi_h, rhi),
                ("row_low", rlo_h, rlo),
            ]
        )
        if flux_mode or name not in FLUX_ONLY
    }
    for load in loads.values():
        load.start()

    barrier = pltpu.get_barrier_semaphore()

    def greet(k, c):
        pl.semaphore_signal(
            barrier, inc=1, device_id=(lax.rem(me + k, DEVS), band), device_id_type=MESH
        )
        return c

    lax.fori_loop(1, DEVS, greet, 0)
    if flux_mode:
        for k in range(1, BANDS):
            pl.semaphore_signal(
                barrier, inc=1, device_id=(me, lax.rem(band + k, BANDS)), device_id_type=MESH
            )
    greeted = DEVS - 1 + (BANDS - 1 if flux_mode else 0)

    if flux_mode:
        x = 2.0 * lax.broadcasted_iota(jnp.int32, (1, CW), 1).astype(F32) / (CW - 1) - 1.0
        loads["coefficients"].wait()
        basis = lax.broadcasted_iota(jnp.int32, (NB, NB), 0) == lax.broadcasted_iota(
            jnp.int32, (NB, NB), 1
        )

        def term(n, p):
            return jnp.sum(
                jnp.where(basis, jnp.broadcast_to(coef[p, n : n + 1, :], (NB, NB)), 0.0),
                axis=1,
                keepdims=True,
            )

        for n in range(CCDS):
            k = [term(n, p) for p in range(6)]
            wk[n, 0] = k[0] + k[1] * x + k[3] * (x * x)
            wk[n, 1] = k[2] + k[4] * x
            wk[n, 2] = jnp.broadcast_to(k[5], (NB, CW))
        loads["column_taps"].wait()

        def column_ops(k, c):
            to = pl.ds(k * CW, CW)
            for n in range(CCDS):
                for p in range(3):
                    m = jnp.zeros((CW, CW), F32)
                    for b in range(3):
                        at = pl.ds((k // 3 * 3 + b) * CW, CW)
                        m = m + cop[at, :] * wk[n, p, pl.ds(3 * k + b, 1), :]
                    high, low = split(m)
                    m_hi[n, to, p * CW : (p + 1) * CW] = high
                    m_lo[n, to, p * CW : (p + 1) * CW] = low
            return c

        for k in range(9):
            column_ops(k, 0)

    loads["patch"].wait()
    lane = lax.broadcasted_iota(jnp.int32, (STRIPS, STRIPS), 1)
    sub = lax.broadcasted_iota(jnp.int32, (STRIPS, STRIPS), 0)
    prow = patch[...]
    pfull = jnp.broadcast_to(prow, (STRIPS, STRIPS))
    pcol = jnp.sum(jnp.where(lane == sub, pfull, 0), axis=1, keepdims=True)
    rank = jnp.sum(
        jnp.where((pcol == pfull) & (sub < lane), 1, 0), axis=0, keepdims=True
    )
    slot = prow * SLOTS + rank
    slot_id = lax.broadcasted_iota(jnp.int32, (DEVS * SLOTS, STRIPS), 0)
    hot[...] = (slot_id == slot).astype(F32).astype(BF16)

    loads["mask"].wait()
    use[...] = jnp.where(jnp.bitwise_and(mask[...], 3) != 3, 1.0, 0.0)
    for name in ("row", "col", "col_scalar", "visit", "variance"):
        loads[name].wait()
    lane1 = lax.broadcasted_iota(jnp.int32, (1, CW), 1)
    sums = jnp.zeros((1, CW), F32)
    usable_count = 0.0
    for c in range(CCDS):
        u = use[c * CH : (c + 1) * CH, :]
        count = jnp.sum(u)
        amount = jnp.sum(u * var[c * CH : (c + 1) * CH, :])
        usable_count = usable_count + count
        v = visit_s[0, c]
        sums = sums + jnp.where(lane1 == v + 16, count, 0.0) + jnp.where(lane1 == v + 24, amount, 0.0)
    strip_lane = lax.broadcasted_iota(jnp.int32, (1, STRIPS), 1)
    vrow = jnp.where(strip_lane < STRIPS // CCDS, visit_s[0, 0], visit_s[0, 1])
    q_sub = lax.broadcasted_iota(jnp.int32, (CW, STRIPS), 0)
    hot_id = lax.broadcasted_iota(jnp.int32, (DEVS, STRIPS), 0)
    meta = jnp.broadcast_to(sums, (DEVS, CW))
    for j in range(SLOTS):
        q = jnp.where(q_sub == 8 * j, row[...], 0)
        q = jnp.where(q_sub == 8 * j + 1, col[...] - COL_SHIFT, q)
        q = jnp.where(q_sub == 8 * j + 2, vrow, q)
        hot_j = (hot_id * SLOTS + j == slot).astype(F32).astype(BF16)
        meta = meta + lax.dot_general(
            hot_j, q.astype(F32).astype(BF16), (((1,), (1,)), ((), ())), preferred_element_type=F32
        )
    msend[...] = meta.reshape(PLANES, GROUP, 1, CW)

    if flux_mode:
        loads["exposures"].wait()
        for c in range(CCDS):
            high, low = split(expo[c * CH : (c + 1) * CH, :])
            e_hi[:, c * CW : (c + 1) * CW] = high
            e_lo[:, c * CW : (c + 1) * CW] = low
        loads["row_high"].wait()
        loads["row_low"].wait()

        def row_pass(k, c):
            at = pl.ds(k * CH, CH)
            to = pl.ds(k * CW, CW)
            s = dot(rhi[at, :], e_hi[...]) + dot(rhi[at, :], e_lo[...]) + dot(rlo[at, :], e_hi[...])
            high, low = split(s)
            for n in range(CCDS):
                s_hi[n, :, to] = high[:, n * CW : (n + 1) * CW]
                s_lo[n, :, to] = low[:, n * CW : (n + 1) * CW]
            return c

        for k in range(9):
            row_pass(k, 0)

    def columns_and_pack():
        y = 2.0 * lax.broadcasted_iota(jnp.int32, (CH, 1), 0).astype(F32) / (CH - 1) - 1.0
        for n in range(CCDS):
            o = dot(s_hi[n], m_hi[n]) + dot(s_hi[n], m_lo[n]) + dot(s_lo[n], m_hi[n])
            first, first_rest = product(y, o[:, CW : 2 * CW])
            second, second_rest = product(y * y, o[:, 2 * CW :])
            conv = (o[:, :CW] + first + second) + (first_rest + second_rest)
            for k in range(CH // SR):
                at = pl.ds(n * CH + k * SR, SR)
                flux = use[at, :] * conv[k * SR : (k + 1) * SR, :]
                tmp[at, :] = pltpu.roll(
                    flux, lax.bitwise_and(col_s[0, n * (CH // SR) + k], CW - 1), 1
                )
        for i in range(SR):
            high, low = split(tmp[pl.ds(i, STRIPS, stride=SR), :])
            packed[pl.ds(i, DEVS * SLOTS, stride=SR), :] = dot(hot[...], high) + dot(hot[...], low)

    early = me < DEVS // 2
    if flux_mode:

        @pl.when(early)
        def _():
            columns_and_pack()

    pl.semaphore_wait(barrier, greeted)

    mine = lax.rem(me, GROUP)
    for k in range(1, PLANES):
        plane = lax.rem(my_plane + k, PLANES)
        pltpu.make_async_remote_copy(
            src_ref=msend.at[plane],
            dst_ref=mrelay.at[my_plane],
            send_sem=send_sem.at[1],
            recv_sem=msem.at[0],
            device_id=(plane * GROUP + mine, band),
            device_id_type=MESH,
        ).start()
    pltpu.make_async_copy(msend.at[my_plane], mrelay.at[my_plane], msem.at[0]).start()

    def relay_meta():
        pltpu.make_async_copy(msend, mrelay, msem.at[0]).wait()
        for k in range(1, GROUP):
            place = lax.rem(mine + k, GROUP)
            pltpu.make_async_remote_copy(
                src_ref=mrelay.at[:, place],
                dst_ref=mrecv.at[:, mine],
                send_sem=send_sem.at[2],
                recv_sem=msem.at[1],
                device_id=(my_plane * GROUP + place, band),
                device_id_type=MESH,
            ).start()
        pltpu.make_async_copy(mrelay.at[:, mine], mrecv.at[:, mine], msem.at[1]).start()

    if flux_mode:

        @pl.when(jnp.logical_not(early))
        def _():
            columns_and_pack()

    else:
        def roll_strip(s, c):
            at = pl.ds(pl.multiple_of(s * SR, SR), SR)
            tmp[at, :] = pltpu.roll(use[at, :], lax.bitwise_and(col_s[0, s], CW - 1), 1)
            return c

        lax.fori_loop(0, STRIPS, roll_strip, 0, unroll=8)
        for i in range(SR):
            high, low = split(tmp[pl.ds(i, STRIPS, stride=SR), :])
            packed[pl.ds(i, DEVS * SLOTS, stride=SR), :] = dot(hot[...], high) + dot(hot[...], low)

    def block(d):
        return pl.ds(pl.multiple_of(d * BLOCK, BLOCK), BLOCK)

    def send_half(half):
        def one(k, c):
            d = half * (DEVS // 2) + lax.rem(me + k, DEVS // 2)

            @pl.when(d != me)
            def _():
                pltpu.make_async_remote_copy(
                    src_ref=packed.at[block(d)],
                    dst_ref=arrived.at[block(me)],
                    send_sem=send_sem.at[0],
                    recv_sem=data_sem.at[my_plane],
                    device_id=(d, band),
                    device_id_type=MESH,
                ).start()

            return c

        lax.fori_loop(0, DEVS // 2, one, 0)

    send_half(0)
    relay_meta()
    send_half(1)
    pltpu.make_async_copy(
        packed.at[block(me)], arrived.at[block(me)], data_sem.at[my_plane]
    ).start()

    def flag_round(r, value, land, mine, peers):
        flag_out[r] = value
        land[mine] = value
        for device_id in peers:
            pltpu.make_async_remote_copy(
                src_ref=flag_out.at[r],
                dst_ref=land.at[mine],
                send_sem=flag_sem.at[0, r],
                recv_sem=flag_sem.at[1, r],
                device_id=device_id,
                device_id_type=MESH,
            ).start()

    def flag_end(r, land):
        n = land.shape[0] - 1
        for k in range(2):
            rest = land.at[pl.ds(0, n)]
            pltpu.make_async_copy(rest, rest, flag_sem.at[k, r]).wait()
        return jnp.max(land[...].reshape(n + 1, CW), axis=0, keepdims=True)

    if flux_mode:
        nonzero = jnp.sum(jnp.where(packed[...] != 0.0, 1.0, 0.0))
        flag = jnp.zeros((1, CW), F32) + (usable_count - nonzero)
        flag_round(
            0, flag, flag_plane, mine,
            [(my_plane * GROUP + lax.rem(mine + k, GROUP), band) for k in range(1, GROUP)],
        )

    pltpu.make_async_copy(mrelay, mrecv, msem.at[1]).wait()
    if flux_mode:
        flag_round(
            1, flag_end(0, flag_plane), flag_z, my_plane,
            [(lax.rem(me + k * GROUP, DEVS), band) for k in range(1, PLANES)],
        )
    got = mrecv[...].reshape(DEVS, CW)
    totals = jnp.sum(got, axis=0, keepdims=True)
    weights = (totals + 1.0) / (pltpu.roll(totals, CW - 8, 1) + 1.0)
    lane_d = lax.broadcasted_iota(jnp.int32, (DEVS, CW), 1)
    for j in range(SLOTS):
        at = pl.ds(j * DEVS, DEVS)
        v = got[:, 8 * j + 2 : 8 * j + 3].astype(jnp.int32)
        vw = jnp.sum(
            jnp.where(lane_d == v + 16, jnp.broadcast_to(weights, (DEVS, CW)), 0.0),
            axis=1,
            keepdims=True,
        )
        rhs[at, 0:CW] = jnp.broadcast_to(got[:, 8 * j + 1 : 8 * j + 2], (DEVS, CW))
        rhs[at, CW : 2 * CW] = jnp.broadcast_to(got[:, 8 * j : 8 * j + 1], (DEVS, CW))
        rhs[at, 2 * CW :] = jnp.broadcast_to(vw, (DEVS, CW))
    spread_in = rhs[...].astype(BF16)
    weights_low = split(rhs[:, 2 * CW :])[1]

    k_sub = lax.broadcasted_iota(jnp.int32, (CHUNK, SLOTS * DEVS), 0)
    k_lane = lax.broadcasted_iota(jnp.int32, (CHUNK, SLOTS * DEVS), 1)
    lane_c = lax.broadcasted_iota(jnp.int32, (CHUNK, CW), 1).astype(F32)
    row_in = (lax.broadcasted_iota(jnp.int32, (CHUNK, CW), 0) % SR).astype(F32)

    def spread(p, c):
        at = pl.ds(pl.multiple_of(p * CHUNK, CHUNK), CHUNK)
        here = (k_lane - p * GROUP == k_sub // BLOCK + (k_sub // SR) % SLOTS * DEVS)
        here = here.astype(F32).astype(BF16)
        full = dot(here, spread_in)
        crep[at, :] = lane_c - (full[:, :CW] + COL_SHIFT)
        rt = (lane_c == full[:, CW : 2 * CW] + row_in).astype(F32)
        turned = jnp.transpose(rt).astype(BF16)
        rows_of[p, :, 0:CHUNK] = turned
        rows_of[p, :, CHUNK : 2 * CHUNK] = turned
        vrep[at, :] = full[:, 2 * CW :] + dot(here, weights_low)
        return c

    lax.fori_loop(0, PLANES, spread, 0)
    if flux_mode:
        flag_round(
            2, flag_end(1, flag_z), flag_band, band,
            [(me, lax.rem(band + k, BANDS)) for k in range(1, BANDS)],
        )

    placed[...] = jnp.zeros_like(placed)

    def place(p, c):
        at = pl.ds(pl.multiple_of(p * CHUNK, CHUNK), CHUNK)
        pltpu.make_async_copy(packed.at[at], arrived.at[at], data_sem.at[p]).wait()
        value = arrived[at, :]
        weight = vrep[at, :]
        maps = [value * weight]
        if flux_mode:
            maps.append(jnp.where(value != 0.0, weight, 0.0))
        off = crep[at, :]
        for n, (high, low) in enumerate(split(m) for m in maps):
            zero = jnp.zeros_like(high)
            for t in range(PW // CW):
                away = off + float(t * CW)
                inside = (away >= 0.0) & (away < CW)
                cols = pl.ds(n * PW + t * CW, CW)
                wide[0:CHUNK, cols] = jnp.where(inside, high, zero)
                wide[CHUNK : 2 * CHUNK, cols] = jnp.where(inside, low, zero)
        placed[...] += dot(rows_of[p], wide[...])
        return c

    lax.fori_loop(0, PLANES, place, 0)
    if flux_mode:
        num_o[...] = placed[:, :PW]
        wgt_o[...] = placed[:, PW:]
        flag_o[...] = flag_end(2, flag_band)
    else:
        wgt_o[...] = placed[...]

    for k in (1, 2):
        others = mrelay.at[pl.ds(0, PLANES - 1)]
        pltpu.make_async_copy(others, others, send_sem.at[k]).wait()
    rest = packed.at[pl.ds(0, (DEVS - 1) * BLOCK)]
    pltpu.make_async_copy(rest, rest, send_sem.at[0]).wait()


def exchange(flux_mode, operands):
    slots = DEVS * BLOCK
    flat = (CCDS * CH, CW)
    hbm = pl.BlockSpec(memory_space=pltpu.HBM)
    vmem = pl.BlockSpec(memory_space=pltpu.VMEM)
    image = jax.ShapeDtypeStruct((PH, PW), F32)
    outs = [image, image, jax.ShapeDtypeStruct((1, CW), F32)] if flux_mode else [image]
    maps = 2 if flux_mode else 1
    return pl.pallas_call(
        functools.partial(kernel, flux_mode),
        out_shape=outs,
        in_specs=[hbm] * 11,
        out_specs=[vmem] * len(outs),
        scratch_shapes=[
            pltpu.VMEM((6, CCDS, NB), F32),
            pltpu.SMEM((1, CCDS), jnp.int32),
            pltpu.VMEM((1, STRIPS), jnp.int32),
            pltpu.VMEM((1, STRIPS), jnp.int32),
            pltpu.VMEM((1, STRIPS), jnp.int32),
            pltpu.SMEM((1, STRIPS), jnp.int32),
            pltpu.VMEM(flat, jnp.int32),
            pltpu.VMEM(flat, F32),
            pltpu.VMEM(flat, F32),
            pltpu.VMEM((9 * CH, CH), BF16),
            pltpu.VMEM((9 * CH, CH), BF16),
            pltpu.VMEM((9 * CW, CW), F32),
            pltpu.VMEM(flat, F32),
            pltpu.VMEM(flat, F32),
            pltpu.VMEM((CH, CCDS * CW), BF16),
            pltpu.VMEM((CH, CCDS * CW), BF16),
            pltpu.VMEM((CCDS, CH, 9 * CW), BF16),
            pltpu.VMEM((CCDS, CH, 9 * CW), BF16),
            pltpu.VMEM((CCDS, 9 * CW, 3 * CW), BF16),
            pltpu.VMEM((CCDS, 9 * CW, 3 * CW), BF16),
            pltpu.VMEM((CCDS, 3, NB, CW), F32),
            pltpu.VMEM((DEVS * SLOTS, STRIPS), BF16),
            pltpu.VMEM((slots, CW), F32),
            pltpu.VMEM((PLANES, GROUP, 1, CW), F32),
            pltpu.VMEM((PLANES, GROUP, 1, CW), F32),
            pltpu.VMEM((slots, CW), F32),
            pltpu.VMEM((PLANES, GROUP, 1, CW), F32),
            pltpu.VMEM((slots, CW), F32),
            pltpu.VMEM((slots, CW), F32),
            pltpu.VMEM((PLANES, PH, 2 * CHUNK), BF16),
            pltpu.VMEM((2 * CHUNK, maps * PW), BF16),
            pltpu.VMEM((SLOTS * DEVS, 3 * CW), F32),
            pltpu.VMEM((PH, maps * PW), F32),
            pltpu.VMEM((3, 1, CW), F32),
            pltpu.VMEM((GROUP, 1, CW), F32),
            pltpu.VMEM((PLANES, 1, CW), F32),
            pltpu.VMEM((BANDS, 1, CW), F32),
            pltpu.SemaphoreType.DMA((12,)),
            pltpu.SemaphoreType.DMA((3,)),
            pltpu.SemaphoreType.DMA((PLANES,)),
            pltpu.SemaphoreType.DMA((2,)),
            pltpu.SemaphoreType.DMA((2, 3)),
        ],
        compiler_params=pltpu.CompilerParams(
            collective_id=0 if flux_mode else 1,
            has_side_effects=True,
            vmem_limit_bytes=40 * 1024 * 1024,
        ),
        cost_estimate=pl.CostEstimate(
            flops=2_600_000_000, bytes_accessed=6_000_000, transcendentals=0
        ),
    )(*(pltpu.with_memory_space_constraint(operand, pltpu.HBM) for operand in operands))


def shards(
    exposures, variance, mask_bits, kernel_coeffs, ccd_visit, strip_patch, strip_row, strip_col
):
    rhi, rlo, cop = tap_matrices()
    flat = (CCDS * CH, CW)
    operands = (
        mask_bits.reshape(flat),
        variance.reshape(flat),
        exposures.reshape(flat),
        kernel_coeffs.transpose(2, 0, 1),
        ccd_visit.reshape(1, CCDS),
        strip_patch.reshape(1, STRIPS),
        strip_row.reshape(1, STRIPS),
        strip_col.reshape(1, STRIPS),
        jnp.asarray(rhi),
        jnp.asarray(rlo),
        jnp.asarray(cop),
    )
    num, wgt, flag = exchange(True, operands)

    def finish(num, wgt):
        return (num / jnp.maximum(wgt, 1.0))[None], jnp.maximum(wgt, 0.0)[None]

    return lax.cond(
        flag[0, 0] > 0.0,
        lambda: finish(num, exchange(False, operands)[0]),
        lambda: finish(num, wgt),
    )


def solution(mesh):
    return jax.shard_map(
        shards,
        mesh=mesh,
        in_specs=(
            P(("band", "patch"), None, None),
            P(("band", "patch"), None, None),
            P(("band", "patch"), None, None),
            P(("band", "patch"), None, None),
            P(("band", "patch"), None),
            P(("band", "patch"), None),
            P(("band", "patch")),
            P(("band", "patch")),
        ),
        out_specs=(P(("band", "patch"), None, None), P(("band", "patch"), None, None)),
        check_vma=False,
    )
```

```python
import functools

import jax
import jax.numpy as jnp
import numpy as np
from jax import lax
from jax.experimental import pallas as pl
from jax.experimental.pallas import tpu as pltpu
from jax.sharding import PartitionSpec as P

PH = 128
PW = 512
KS = 21
VISITS = 8
GAUSS_WIDTHS = (0.75, 1.5, 3.0)
MESH = pl.DeviceIdType.MESH
F32 = jnp.float32
BF16 = jnp.bfloat16

CCDS = 2
CH = 256
CW = 128
SR = 8
STRIPS = 64
DEVS = 64
NB = 27
SLOTS = 2
BLOCK = SLOTS * SR
PLANES = 8
GROUP = DEVS // PLANES
BANDS = 4
FLUX_ONLY = ("exposures", "row_high", "row_low", "coefficients", "column_taps")
CHUNK = GROUP * BLOCK
COL_SHIFT = 192


def taps(offsets):
    half = KS // 2
    support = np.arange(-half, half + 1, dtype=np.float64)
    inside = np.abs(offsets) <= half
    tables = []
    for spread in GAUSS_WIDTHS:
        total = np.sum(np.exp(-support * support / (2.0 * spread * spread)))
        profile = np.where(inside, np.exp(-offsets * offsets / (2.0 * spread * spread)) / total, 0.0)
        scaled = offsets / spread
        tables += [profile, profile * scaled, profile * scaled * scaled]
    return np.stack(tables)


def tap_matrices():
    rows = np.arange(CH, dtype=np.float64)
    row_ops = taps(rows[None, :] - rows[:, None]).astype(np.float32).reshape(9 * CH, CH)
    cols = np.arange(CW, dtype=np.float64)
    col_ops = taps(cols[:, None] - cols[None, :]).astype(np.float32).reshape(9 * CW, CW)
    high = row_ops.astype(BF16)
    low = (row_ops - high.astype(np.float32)).astype(BF16)
    return high, low, col_ops


def split(x):
    high = x.astype(BF16)
    return high, (x - high.astype(F32)).astype(BF16)


def halves(x):
    scaled = x * 4097.0
    high = scaled - (scaled - x)
    return high, x - high


def product(a, b):
    p = a * b
    a_high, a_low = halves(a)
    b_high, b_low = halves(b)
    return p, ((a_high * b_high - p) + a_high * b_low + a_low * b_high) + a_low * b_low


def dot(a, b):
    return jnp.dot(a, b, preferred_element_type=F32)


def kernel(
    flux_mode,
    mask_h, var_h, exp_h, coef_h, visit_h, patch_h, row_h, col_h, rhi_h, rlo_h, cop_h,
    *refs,
):
    if flux_mode:
        num_o, wgt_o, flag_o, *refs = refs
    else:
        wgt_o, *refs = refs
    (
        coef, visit_s, patch, row, col, col_s, mask, var, expo, rhi, rlo, cop,
        use, tmp, e_hi, e_lo, s_hi, s_lo, m_hi, m_lo, wk,
        hot, packed, msend, mrelay, arrived, mrecv, crep, vrep, rows_of, wide, rhs, placed,
        flag_out, flag_plane, flag_z, flag_band,
        load_sem, send_sem, data_sem, msem, flag_sem,
    ) = refs
    me = lax.axis_index("patch")
    band = lax.axis_index("band")
    my_plane = me // GROUP

    loads = {
        name: pltpu.make_async_copy(src, dst, load_sem.at[k])
        for k, (name, src, dst) in enumerate(
            [
                ("coefficients", coef_h, coef),
                ("column_taps", cop_h, cop),
                ("patch", patch_h, patch),
                ("mask", mask_h, mask),
                ("row", row_h, row),
                ("col", col_h, col),
                ("visit", visit_h, visit_s),
                ("col_scalar", col_h, col_s),
                ("variance", var_h, var),
                ("exposures", exp_h, expo),
                ("row_high", rhi_h, rhi),
                ("row_low", rlo_h, rlo),
            ]
        )
        if flux_mode or name not in FLUX_ONLY
    }
    for load in loads.values():
        load.start()

    barrier = pltpu.get_barrier_semaphore()

    def greet(k, c):
        pl.semaphore_signal(
            barrier, inc=1, device_id=(lax.rem(me + k, DEVS), band), device_id_type=MESH
        )
        return c

    lax.fori_loop(1, DEVS, greet, 0)
    if flux_mode:
        for k in range(1, BANDS):
            pl.semaphore_signal(
                barrier, inc=1, device_id=(me, lax.rem(band + k, BANDS)), device_id_type=MESH
            )
    greeted = DEVS - 1 + (BANDS - 1 if flux_mode else 0)

    if flux_mode:
        x = 2.0 * lax.broadcasted_iota(jnp.int32, (1, CW), 1).astype(F32) / (CW - 1) - 1.0
        loads["coefficients"].wait()
        basis = lax.broadcasted_iota(jnp.int32, (NB, NB), 0) == lax.broadcasted_iota(
            jnp.int32, (NB, NB), 1
        )

        def term(n, p):
            return jnp.sum(
                jnp.where(basis, jnp.broadcast_to(coef[p, n : n + 1, :], (NB, NB)), 0.0),
                axis=1,
                keepdims=True,
            )

        for n in range(CCDS):
            k = [term(n, p) for p in range(6)]
            wk[n, 0] = k[0] + k[1] * x + k[3] * (x * x)
            wk[n, 1] = k[2] + k[4] * x
            wk[n, 2] = jnp.broadcast_to(k[5], (NB, CW))
        loads["column_taps"].wait()

        def column_ops(k, c):
            to = pl.ds(k * CW, CW)
            for n in range(CCDS):
                for p in range(3):
                    m = jnp.zeros((CW, CW), F32)
                    for b in range(3):
                        at = pl.ds((k // 3 * 3 + b) * CW, CW)
                        m = m + cop[at, :] * wk[n, p, pl.ds(3 * k + b, 1), :]
                    high, low = split(m)
                    m_hi[n, to, p * CW : (p + 1) * CW] = high
                    m_lo[n, to, p * CW : (p + 1) * CW] = low
            return c

        for k in range(9):
            column_ops(k, 0)

    loads["patch"].wait()
    lane = lax.broadcasted_iota(jnp.int32, (STRIPS, STRIPS), 1)
    sub = lax.broadcasted_iota(jnp.int32, (STRIPS, STRIPS), 0)
    prow = patch[...]
    pfull = jnp.broadcast_to(prow, (STRIPS, STRIPS))
    pcol = jnp.sum(jnp.where(lane == sub, pfull, 0), axis=1, keepdims=True)
    rank = jnp.sum(
        jnp.where((pcol == pfull) & (sub < lane), 1, 0), axis=0, keepdims=True
    )
    slot = prow * SLOTS + rank
    slot_id = lax.broadcasted_iota(jnp.int32, (DEVS * SLOTS, STRIPS), 0)
    hot[...] = (slot_id == slot).astype(F32).astype(BF16)

    loads["mask"].wait()
    use[...] = jnp.where(jnp.bitwise_and(mask[...], 3) != 3, 1.0, 0.0)
    for name in ("row", "col", "col_scalar", "visit", "variance"):
        loads[name].wait()
    lane1 = lax.broadcasted_iota(jnp.int32, (1, CW), 1)
    sums = jnp.zeros((1, CW), F32)
    usable_count = 0.0
    for c in range(CCDS):
        u = use[c * CH : (c + 1) * CH, :]
        count = jnp.sum(u)
        amount = jnp.sum(u * var[c * CH : (c + 1) * CH, :])
        usable_count = usable_count + count
        v = visit_s[0, c]
        sums = sums + jnp.where(lane1 == v + 16, count, 0.0) + jnp.where(lane1 == v + 24, amount, 0.0)
    strip_lane = lax.broadcasted_iota(jnp.int32, (1, STRIPS), 1)
    vrow = jnp.where(strip_lane < STRIPS // CCDS, visit_s[0, 0], visit_s[0, 1])
    q_sub = lax.broadcasted_iota(jnp.int32, (CW, STRIPS), 0)
    hot_id = lax.broadcasted_iota(jnp.int32, (DEVS, STRIPS), 0)
    meta = jnp.broadcast_to(sums, (DEVS, CW))
    for j in range(SLOTS):
        q = jnp.where(q_sub == 8 * j, row[...], 0)
        q = jnp.where(q_sub == 8 * j + 1, col[...] - COL_SHIFT, q)
        q = jnp.where(q_sub == 8 * j + 2, vrow, q)
        hot_j = (hot_id * SLOTS + j == slot).astype(F32).astype(BF16)
        meta = meta + lax.dot_general(
            hot_j, q.astype(F32).astype(BF16), (((1,), (1,)), ((), ())), preferred_element_type=F32
        )
    msend[...] = meta.reshape(PLANES, GROUP, 1, CW)

    if flux_mode:
        loads["exposures"].wait()
        for c in range(CCDS):
            high, low = split(expo[c * CH : (c + 1) * CH, :])
            e_hi[:, c * CW : (c + 1) * CW] = high
            e_lo[:, c * CW : (c + 1) * CW] = low
        loads["row_high"].wait()
        loads["row_low"].wait()

        def row_pass(k, c):
            at = pl.ds(k * CH, CH)
            to = pl.ds(k * CW, CW)
            s = dot(rhi[at, :], e_hi[...]) + dot(rhi[at, :], e_lo[...]) + dot(rlo[at, :], e_hi[...])
            high, low = split(s)
            for n in range(CCDS):
                s_hi[n, :, to] = high[:, n * CW : (n + 1) * CW]
                s_lo[n, :, to] = low[:, n * CW : (n + 1) * CW]
            return c

        for k in range(9):
            row_pass(k, 0)

    def columns_and_pack():
        y = 2.0 * lax.broadcasted_iota(jnp.int32, (CH, 1), 0).astype(F32) / (CH - 1) - 1.0
        for n in range(CCDS):
            o = dot(s_hi[n], m_hi[n]) + dot(s_hi[n], m_lo[n]) + dot(s_lo[n], m_hi[n])
            first, first_rest = product(y, o[:, CW : 2 * CW])
            second, second_rest = product(y * y, o[:, 2 * CW :])
            conv = (o[:, :CW] + first + second) + (first_rest + second_rest)
            for k in range(CH // SR):
                at = pl.ds(n * CH + k * SR, SR)
                flux = use[at, :] * conv[k * SR : (k + 1) * SR, :]
                tmp[at, :] = pltpu.roll(
                    flux, lax.bitwise_and(col_s[0, n * (CH // SR) + k], CW - 1), 1
                )
        for i in range(SR):
            high, low = split(tmp[pl.ds(i, STRIPS, stride=SR), :])
            packed[pl.ds(i, DEVS * SLOTS, stride=SR), :] = dot(hot[...], high) + dot(hot[...], low)

    early = me < DEVS // 2
    if flux_mode:

        @pl.when(early)
        def _():
            columns_and_pack()

    pl.semaphore_wait(barrier, greeted)

    mine = lax.rem(me, GROUP)
    for k in range(1, PLANES):
        plane = lax.rem(my_plane + k, PLANES)
        pltpu.make_async_remote_copy(
            src_ref=msend.at[plane],
            dst_ref=mrelay.at[my_plane],
            send_sem=send_sem.at[1],
            recv_sem=msem.at[0],
            device_id=(plane * GROUP + mine, band),
            device_id_type=MESH,
        ).start()
    pltpu.make_async_copy(msend.at[my_plane], mrelay.at[my_plane], msem.at[0]).start()

    def relay_meta():
        pltpu.make_async_copy(msend, mrelay, msem.at[0]).wait()
        for k in range(1, GROUP):
            place = lax.rem(mine + k, GROUP)
            pltpu.make_async_remote_copy(
                src_ref=mrelay.at[:, place],
                dst_ref=mrecv.at[:, mine],
                send_sem=send_sem.at[2],
                recv_sem=msem.at[1],
                device_id=(my_plane * GROUP + place, band),
                device_id_type=MESH,
            ).start()
        pltpu.make_async_copy(mrelay.at[:, mine], mrecv.at[:, mine], msem.at[1]).start()

    if flux_mode:

        @pl.when(jnp.logical_not(early))
        def _():
            columns_and_pack()

    else:
        def roll_strip(s, c):
            at = pl.ds(pl.multiple_of(s * SR, SR), SR)
            tmp[at, :] = pltpu.roll(use[at, :], lax.bitwise_and(col_s[0, s], CW - 1), 1)
            return c

        lax.fori_loop(0, STRIPS, roll_strip, 0, unroll=8)
        for i in range(SR):
            high, low = split(tmp[pl.ds(i, STRIPS, stride=SR), :])
            packed[pl.ds(i, DEVS * SLOTS, stride=SR), :] = dot(hot[...], high) + dot(hot[...], low)

    def block(d):
        return pl.ds(pl.multiple_of(d * BLOCK, BLOCK), BLOCK)

    def send_half(half):
        def one(k, c):
            d = half * (DEVS // 2) + lax.rem(me + k, DEVS // 2)

            @pl.when(d != me)
            def _():
                pltpu.make_async_remote_copy(
                    src_ref=packed.at[block(d)],
                    dst_ref=arrived.at[block(me)],
                    send_sem=send_sem.at[0],
                    recv_sem=data_sem.at[my_plane],
                    device_id=(d, band),
                    device_id_type=MESH,
                ).start()

            return c

        lax.fori_loop(0, DEVS // 2, one, 0)

    send_half(0)
    relay_meta()
    send_half(1)
    pltpu.make_async_copy(
        packed.at[block(me)], arrived.at[block(me)], data_sem.at[my_plane]
    ).start()

    def flag_round(r, value, land, mine, peers):
        flag_out[r] = value
        land[mine] = value
        for device_id in peers:
            pltpu.make_async_remote_copy(
                src_ref=flag_out.at[r],
                dst_ref=land.at[mine],
                send_sem=flag_sem.at[0, r],
                recv_sem=flag_sem.at[1, r],
                device_id=device_id,
                device_id_type=MESH,
            ).start()

    def flag_end(r, land):
        n = land.shape[0] - 1
        for k in range(2):
            rest = land.at[pl.ds(0, n)]
            pltpu.make_async_copy(rest, rest, flag_sem.at[k, r]).wait()
        return jnp.max(land[...].reshape(n + 1, CW), axis=0, keepdims=True)

    if flux_mode:
        nonzero = jnp.sum(jnp.where(packed[...] != 0.0, 1.0, 0.0))
        flag = jnp.zeros((1, CW), F32) + (usable_count - nonzero)
        flag_round(
            0, flag, flag_plane, mine,
            [(my_plane * GROUP + lax.rem(mine + k, GROUP), band) for k in range(1, GROUP)],
        )

    pltpu.make_async_copy(mrelay, mrecv, msem.at[1]).wait()
    if flux_mode:
        flag_round(
            1, flag_end(0, flag_plane), flag_z, my_plane,
            [(lax.rem(me + k * GROUP, DEVS), band) for k in range(1, PLANES)],
        )
    got = mrecv[...].reshape(DEVS, CW)
    totals = jnp.sum(got, axis=0, keepdims=True)
    weights = (totals + 1.0) / (pltpu.roll(totals, CW - 8, 1) + 1.0)
    lane_d = lax.broadcasted_iota(jnp.int32, (DEVS, CW), 1)
    for j in range(SLOTS):
        at = pl.ds(j * DEVS, DEVS)
        v = got[:, 8 * j + 2 : 8 * j + 3].astype(jnp.int32)
        vw = jnp.sum(
            jnp.where(lane_d == v + 16, jnp.broadcast_to(weights, (DEVS, CW)), 0.0),
            axis=1,
            keepdims=True,
        )
        rhs[at, 0:CW] = jnp.broadcast_to(got[:, 8 * j + 1 : 8 * j + 2], (DEVS, CW))
        rhs[at, CW : 2 * CW] = jnp.broadcast_to(got[:, 8 * j : 8 * j + 1], (DEVS, CW))
        rhs[at, 2 * CW :] = jnp.broadcast_to(vw, (DEVS, CW))
    spread_in = rhs[...].astype(BF16)
    weights_low = split(rhs[:, 2 * CW :])[1]

    k_sub = lax.broadcasted_iota(jnp.int32, (CHUNK, SLOTS * DEVS), 0)
    k_lane = lax.broadcasted_iota(jnp.int32, (CHUNK, SLOTS * DEVS), 1)
    lane_c = lax.broadcasted_iota(jnp.int32, (CHUNK, CW), 1).astype(F32)
    row_in = (lax.broadcasted_iota(jnp.int32, (CHUNK, CW), 0) % SR).astype(F32)

    def spread(p, c):
        at = pl.ds(pl.multiple_of(p * CHUNK, CHUNK), CHUNK)
        here = (k_lane - p * GROUP == k_sub // BLOCK + (k_sub // SR) % SLOTS * DEVS)
        here = here.astype(F32).astype(BF16)
        full = dot(here, spread_in)
        crep[at, :] = lane_c - (full[:, :CW] + COL_SHIFT)
        rt = (lane_c == full[:, CW : 2 * CW] + row_in).astype(F32)
        turned = jnp.transpose(rt).astype(BF16)
        rows_of[p, :, 0:CHUNK] = turned
        rows_of[p, :, CHUNK : 2 * CHUNK] = turned
        vrep[at, :] = full[:, 2 * CW :] + dot(here, weights_low)
        return c

    lax.fori_loop(0, PLANES, spread, 0)
    if flux_mode:
        flag_round(
            2, flag_end(1, flag_z), flag_band, band,
            [(me, lax.rem(band + k, BANDS)) for k in range(1, BANDS)],
        )

    placed[...] = jnp.zeros_like(placed)

    def place(pair, c):
        total = 0.0
        for m in range(2):
            at = pl.ds(pl.multiple_of((2 * pair + m) * CHUNK, CHUNK), CHUNK)
            pltpu.make_async_copy(
                packed.at[at], arrived.at[at], data_sem.at[2 * pair + m]
            ).wait()
        for m in range(2):
            p = 2 * pair + m
            at = pl.ds(pl.multiple_of(p * CHUNK, CHUNK), CHUNK)
            value = arrived[at, :]
            weight = vrep[at, :]
            maps = [value * weight]
            if flux_mode:
                maps.append(jnp.where(value != 0.0, weight, 0.0))
            off = crep[at, :]
            for n, (high, low) in enumerate(split(v) for v in maps):
                zero = jnp.zeros_like(high)
                for t in range(PW // CW):
                    away = off + float(t * CW)
                    inside = (away >= 0.0) & (away < CW)
                    cols = pl.ds(n * PW + t * CW, CW)
                    wide[m, 0:CHUNK, cols] = jnp.where(inside, high, zero)
                    wide[m, CHUNK : 2 * CHUNK, cols] = jnp.where(inside, low, zero)
            total = total + dot(rows_of[p], wide[m])
        placed[...] += total
        return c

    lax.fori_loop(0, PLANES // 2, place, 0)
    if flux_mode:
        num_o[...] = placed[:, :PW]
        wgt_o[...] = placed[:, PW:]
        flag_o[...] = flag_end(2, flag_band)
    else:
        wgt_o[...] = placed[...]

    for k in (1, 2):
        others = mrelay.at[pl.ds(0, PLANES - 1)]
        pltpu.make_async_copy(others, others, send_sem.at[k]).wait()
    rest = packed.at[pl.ds(0, (DEVS - 1) * BLOCK)]
    pltpu.make_async_copy(rest, rest, send_sem.at[0]).wait()


def exchange(flux_mode, operands):
    slots = DEVS * BLOCK
    flat = (CCDS * CH, CW)
    hbm = pl.BlockSpec(memory_space=pltpu.HBM)
    vmem = pl.BlockSpec(memory_space=pltpu.VMEM)
    image = jax.ShapeDtypeStruct((PH, PW), F32)
    outs = [image, image, jax.ShapeDtypeStruct((1, CW), F32)] if flux_mode else [image]
    maps = 2 if flux_mode else 1
    return pl.pallas_call(
        functools.partial(kernel, flux_mode),
        out_shape=outs,
        in_specs=[hbm] * 11,
        out_specs=[vmem] * len(outs),
        scratch_shapes=[
            pltpu.VMEM((6, CCDS, NB), F32),
            pltpu.SMEM((1, CCDS), jnp.int32),
            pltpu.VMEM((1, STRIPS), jnp.int32),
            pltpu.VMEM((1, STRIPS), jnp.int32),
            pltpu.VMEM((1, STRIPS), jnp.int32),
            pltpu.SMEM((1, STRIPS), jnp.int32),
            pltpu.VMEM(flat, jnp.int32),
            pltpu.VMEM(flat, F32),
            pltpu.VMEM(flat, F32),
            pltpu.VMEM((9 * CH, CH), BF16),
            pltpu.VMEM((9 * CH, CH), BF16),
            pltpu.VMEM((9 * CW, CW), F32),
            pltpu.VMEM(flat, F32),
            pltpu.VMEM(flat, F32),
            pltpu.VMEM((CH, CCDS * CW), BF16),
            pltpu.VMEM((CH, CCDS * CW), BF16),
            pltpu.VMEM((CCDS, CH, 9 * CW), BF16),
            pltpu.VMEM((CCDS, CH, 9 * CW), BF16),
            pltpu.VMEM((CCDS, 9 * CW, 3 * CW), BF16),
            pltpu.VMEM((CCDS, 9 * CW, 3 * CW), BF16),
            pltpu.VMEM((CCDS, 3, NB, CW), F32),
            pltpu.VMEM((DEVS * SLOTS, STRIPS), BF16),
            pltpu.VMEM((slots, CW), F32),
            pltpu.VMEM((PLANES, GROUP, 1, CW), F32),
            pltpu.VMEM((PLANES, GROUP, 1, CW), F32),
            pltpu.VMEM((slots, CW), F32),
            pltpu.VMEM((PLANES, GROUP, 1, CW), F32),
            pltpu.VMEM((slots, CW), F32),
            pltpu.VMEM((slots, CW), F32),
            pltpu.VMEM((PLANES, PH, 2 * CHUNK), BF16),
            pltpu.VMEM((2, 2 * CHUNK, maps * PW), BF16),
            pltpu.VMEM((SLOTS * DEVS, 3 * CW), F32),
            pltpu.VMEM((PH, maps * PW), F32),
            pltpu.VMEM((3, 1, CW), F32),
            pltpu.VMEM((GROUP, 1, CW), F32),
            pltpu.VMEM((PLANES, 1, CW), F32),
            pltpu.VMEM((BANDS, 1, CW), F32),
            pltpu.SemaphoreType.DMA((12,)),
            pltpu.SemaphoreType.DMA((3,)),
            pltpu.SemaphoreType.DMA((PLANES,)),
            pltpu.SemaphoreType.DMA((2,)),
            pltpu.SemaphoreType.DMA((2, 3)),
        ],
        compiler_params=pltpu.CompilerParams(
            collective_id=0 if flux_mode else 1,
            has_side_effects=True,
            vmem_limit_bytes=40 * 1024 * 1024,
        ),
        cost_estimate=pl.CostEstimate(
            flops=2_600_000_000, bytes_accessed=6_000_000, transcendentals=0
        ),
    )(*(pltpu.with_memory_space_constraint(operand, pltpu.HBM) for operand in operands))


def shards(
    exposures, variance, mask_bits, kernel_coeffs, ccd_visit, strip_patch, strip_row, strip_col
):
    rhi, rlo, cop = tap_matrices()
    flat = (CCDS * CH, CW)
    operands = (
        mask_bits.reshape(flat),
        variance.reshape(flat),
        exposures.reshape(flat),
        kernel_coeffs.transpose(2, 0, 1),
        ccd_visit.reshape(1, CCDS),
        strip_patch.reshape(1, STRIPS),
        strip_row.reshape(1, STRIPS),
        strip_col.reshape(1, STRIPS),
        jnp.asarray(rhi),
        jnp.asarray(rlo),
        jnp.asarray(cop),
    )
    num, wgt, flag = exchange(True, operands)

    def finish(num, wgt):
        return (num / jnp.maximum(wgt, 1.0))[None], jnp.maximum(wgt, 0.0)[None]

    return lax.cond(
        flag[0, 0] > 0.0,
        lambda: finish(num, exchange(False, operands)[0]),
        lambda: finish(num, wgt),
    )


def solution(mesh):
    return jax.shard_map(
        shards,
        mesh=mesh,
        in_specs=(
            P(("band", "patch"), None, None),
            P(("band", "patch"), None, None),
            P(("band", "patch"), None, None),
            P(("band", "patch"), None, None),
            P(("band", "patch"), None),
            P(("band", "patch"), None),
            P(("band", "patch")),
            P(("band", "patch")),
        ),
        out_specs=(P(("band", "patch"), None, None), P(("band", "patch"), None, None)),
        check_vma=False,
    )
```
